128 devices in a mesh: row: 16 (over y_lo, x, core), col: 8 (over z, y_hi).
Axes of the slice: x: 4, y: 4 (y_hi: 2, y_lo: 2; y = y_hi * 2 + y_lo), z: 4, core: 2. Of those that a mesh axis runs over, the one named last changes fastest.
Arguments:
- integrals: bfloat16 [65536, 2048], P(('row', 'col')), may hold values from -6 to 6
- occupied: bfloat16 [256, 256], replicated, may hold values from -0.375 to 0.375
- virtual: bfloat16 [256, 256], replicated, may hold values from -0.375 to 0.375
- pair_mask: int32 [16, 32], replicated, may hold values 0 or 1
- green_mask: int32 [2, 4, 4], replicated, may hold values 0 or 1
Outputs:
- polarizability: float32 [2048, 2048], P(('row', 'col'))
The draws below stay inside these ranges and needn't reach their ends.
All inputs are finite; a program needn't handle non-finite values.
Results may differ from the reference program's by a relative error of at most 0.0041.
Values may be sent and summed in bfloat16 or wider, within the bound.
A program may use at most 64 MiB of HBM per device.

```python
import jax
import jax.numpy as jnp
from jax import lax

BLK = 64
NBLK = 4
NPB = 32
NB = 256
NP = 2048


def plant(entries, key, low, largest):
    dims = entries.shape
    spot = [jax.random.randint(jax.random.fold_in(key, axis), (), 0, dims[axis]) for axis in range(len(dims))]
    entries = entries.at[tuple(spot)].set(low)
    longest = dims.index(max(dims))
    spot[longest] = (spot[longest] + 1) % dims[longest]
    return entries.at[tuple(spot)].set(largest)


def block_scale(own_key, extent, pieces, low, top_value):
    def one(position, shards_of):
        steps = jax.random.uniform(jax.random.fold_in(jax.random.fold_in(own_key, 6), position), (shards_of,), jnp.float32, low / len(pieces), top_value / len(pieces))
        return jnp.repeat(jnp.exp(steps), extent[position] // shards_of).reshape((-1,) + (1,) * (len(extent) - position - 1))

    gain = one(*pieces[0])
    for cut in pieces[1:]:
        gain = gain * one(*cut)
    return gain


def noise(rng, dims, spread, bound, pieces=(), held_as=jnp.bfloat16):
    array = spread * jax.random.normal(rng, dims, jnp.float32)
    if pieces:
        array = array * block_scale(rng, dims, pieces, -0.22, 0.18)
    return jnp.clip(array, -bound, bound).astype(held_as)


def setup_inputs(seed: int = 0) -> dict:
    keys = jax.random.split(jax.random.key(seed), 6)
    integrals = noise(keys[0], (NB * NB, NP), 1.0, 6.0, ((0, 128),))
    occupied = noise(keys[1], (NB, NB), NB ** -0.5, 0.375)
    virtual = noise(keys[2], (NB, NB), NB ** -0.5, 0.375)
    pair_mask = plant((jax.random.randint(keys[3], (NBLK * NBLK, NPB), 0, 4) < 3).astype(jnp.int32), jax.random.fold_in(keys[3], 1), 0, 1)
    green_mask = plant((jax.random.randint(keys[4], (2, NBLK, NBLK), 0, 4) < 3).astype(jnp.int32), jax.random.fold_in(keys[4], 1), 0, 1)
    return {"integrals": integrals, "occupied": occupied, "virtual": virtual, "pair_mask": pair_mask, "green_mask": green_mask}


def mask_green(green, green_gate):
    scaled = green.reshape(NBLK, BLK, NBLK, BLK) * green_gate.astype(green.dtype)[:, None, :, None]
    return scaled.reshape(NB, NB)


def reference(integrals, occupied, virtual, pair_mask, green_mask):
    block_table = pair_mask.reshape(NBLK, NBLK, NPB).astype(integrals.dtype)
    masked = (integrals.reshape(NBLK, BLK, NBLK, BLK, NPB, BLK) * block_table[:, None, :, None, :, None]).reshape(NB * NB, NP)
    occ_wide = mask_green(occupied, green_mask[0]).astype(jnp.float32)
    virt_wide = mask_green(virtual, green_mask[1]).astype(jnp.float32)

    def one_block(start):
        block_piece = lax.dynamic_slice_in_dim(masked, start, BLK, 1).reshape(NB, NB, BLK).astype(jnp.float32)
        half_done = jnp.einsum('mnp,ns->msp', block_piece, virt_wide).astype(jnp.bfloat16)
        both_done = jnp.einsum('lm,msp->lsp', occ_wide, half_done.astype(jnp.float32)).astype(jnp.bfloat16)
        return jnp.dot(both_done.reshape(NB * NB, BLK).T, masked, preferred_element_type=jnp.float32)

    starts = (jnp.arange(NPB) * BLK).astype(jnp.int32)
    row_blocks = lax.map(one_block, starts)
    return row_blocks.reshape(NP, NP) / NB
```

```python
import functools

import jax
import jax.numpy as jnp
from jax import lax
from jax.experimental import pallas as pl
from jax.experimental.pallas import tpu as pltpu
from jax.sharding import PartitionSpec as P

F32 = jnp.float32
BF16 = jnp.bfloat16
MESH = pl.DeviceIdType.MESH
CW = 512
QW = 256
NU = 8
DIMS = ("ylo", "x", "z", "yhi")
SIZE = {"ylo": 2, "x": 4, "z": 4, "yhi": 2}
ORDERS = (("x", "y", "z"), ("y", "z", "x"), ("z", "x", "y"))


def parts_of(axis):
    return ("ylo", "yhi") if axis == "y" else (axis,)


def left_after(dims, axis):
    return tuple(d for d in dims if d not in parts_of(axis))


def pick(dims, axis, k):
    at = {"x": k, "z": k} if axis != "y" else {"ylo": k % 2, "yhi": k // 2}
    return tuple(at[d] if d in parts_of(axis) else slice(None) for d in dims)


def shape_of(dims):
    return tuple(SIZE[d] for d in dims)


def device(pos, core):
    return ((pos["y"] % 2) * 8 + pos["x"] * 2 + core, pos["z"] * 2 + pos["y"] // 2)


def iota(shape, axis):
    return lax.broadcasted_iota(jnp.int32, shape, axis)


def kernel(
    ints, occ, virt, pair_gate, green_gate, out,
    mx, gate, vt, perm, hd, hsend, msend, hrecv, mall, spread, occ_t, wide, both_t,
    send_a, recv_a, recv_c, *rest,
):
    acc_a, acc_b, recv_b = rest[:NU], rest[NU : 2 * NU], rest[2 * NU : 3 * NU]
    x_own, x_send, x_recv, h_send, h_recv, m_send, m_recv, p_send, p_recv, r_send, r_recv = rest[3 * NU :]
    row, col = lax.axis_index("row"), lax.axis_index("col")
    core = row % 2
    me = {"x": (row // 2) % 4, "y": (col % 2) * 2 + row // 8, "z": col // 2}
    chip = (row // 2) * 8 + col
    partner = (row - core + (1 - core), col)

    def other(i):
        pos = {
            "x": (me["x"] + i) % 4,
            "y": (me["y"] + i + i // 4) % 4,
            "z": (me["z"] + i + i // 16) % 4,
        }
        return pos

    def chip_of(pos):
        return ((pos["y"] % 2) * 4 + pos["x"]) * 8 + pos["z"] * 2 + pos["y"] // 2

    barrier = pltpu.get_barrier_semaphore()
    pl.semaphore_signal(barrier, inc=1, device_id=partner, device_id_type=MESH)

    @pl.loop(1, 64)
    def _(i):
        pl.semaphore_signal(barrier, inc=1, device_id=device(other(i), core), device_id_type=MESH)

    def tile(t, c):
        return pl.ds(pl.multiple_of((2 * t + c) * 128, 128), 128)

    own = []
    for ch in range(2):
        for t in range(4):
            cp = pltpu.make_async_copy(
                ints.at[:, :, tile(4 * ch + t, core)],
                mx.at[pl.ds(2 * core, 2), :, pl.ds(ch * CW + t * 128, 128)],
                x_own.at[ch, t],
            )
            cp.start()
            own.append(cp)

    lane = iota((1, 128), 1)
    for g in range(4):
        for t in range(8):
            a = pair_gate[(row // 4) * 4 + g, 4 * t + 2 * core].astype(F32)
            b = pair_gate[(row // 4) * 4 + g, 4 * t + 2 * core + 1].astype(F32)
            gate[g : g + 1, t * 128 : (t + 1) * 128] = jnp.where(lane < 64, a, b)
    lane = iota((1, 256), 1)

    def gated(ref, which):
        blocks = []
        for a in range(4):
            line = jnp.zeros((1, 256), F32)
            for b in range(4):
                line = jnp.where(lane // 64 == b, green_gate[which, a, b].astype(F32), line)
            blocks.append(ref[64 * a : 64 * a + 64, :].astype(F32) * line)
        return jnp.concatenate(blocks, axis=0)

    vt[...] = gated(virt, 1).T.astype(BF16)
    r, c = iota((256, 256), 0), iota((256, 256), 1)
    perm[...] = (c == ((r // 4) % 4) * 64 + (r // 16) * 4 + r % 4).astype(F32).astype(BF16)

    pl.semaphore_wait(barrier, 64)
    theirs = []
    for ch in range(2):
        for t in range(4):
            cp = pltpu.make_async_remote_copy(
                src_ref=ints.at[:, :, tile(4 * ch + t, 1 - core)],
                dst_ref=mx.at[pl.ds(2 * core, 2), :, pl.ds(ch * CW + t * 128, 128)],
                send_sem=x_send.at[ch, t],
                recv_sem=x_recv.at[ch, t],
                device_id=partner,
                device_id_type=MESH,
            )
            cp.start()
            theirs.append(cp)

    def send_all(src, dst, send_sem, recv_sem):
        @pl.loop(1, 64)
        def _(i):
            pos = other(i)
            pltpu.make_async_remote_copy(
                src_ref=src.at[chip_of(pos)],
                dst_ref=dst.at[chip],
                send_sem=send_sem,
                recv_sem=recv_sem,
                device_id=device(pos, core),
                device_id_type=MESH,
            ).start()

        dst[chip] = src[chip]

    def wait_all(ref, sem):
        pltpu.make_async_copy(ref.at[pl.ds(0, 63)], ref.at[pl.ds(0, 63)], sem).wait()

    for ch in range(2):
        for t in range(4):
            own[4 * ch + t].wait()
            theirs[4 * ch + t].wait_recv()
        for piece in range(CW // QW):
            lanes = pl.ds(ch * CW + piece * QW, QW)
            part = pl.ds(piece * QW, QW)

            @pl.loop(0, 4)
            def _(k):
                for g in range(4):
                    rows = pl.ds(64 * g, 64)
                    mx[k, rows, lanes] = (mx[k, rows, lanes].astype(F32) * gate[g : g + 1, lanes]).astype(BF16)
                hd[k, :, part] = jnp.dot(vt[...], mx[k, :, lanes], preferred_element_type=F32).astype(BF16)

            for g in range(4):
                rows = pl.ds(64 * g, 64)
                got = jnp.dot(perm[...], hd[:, rows, part].reshape(256, QW), preferred_element_type=F32)
                hsend[ch, pl.ds(16 * g, 16), :, part] = got.astype(BF16).reshape(16, 16, QW)
        send_all(hsend.at[ch], hrecv.at[ch], h_send.at[ch], h_recv.at[ch])
    for ch in range(2):
        for piece in range(CW // QW):
            lanes = pl.ds(ch * CW + piece * QW, QW)
            part = pl.ds(piece * QW, QW)
            for g in range(4):
                rows = pl.ds(64 * g, 64)
                got = jnp.dot(perm[...], mx[:, rows, lanes].reshape(256, QW), preferred_element_type=F32)
                msend[ch, pl.ds(16 * g, 16), :, part] = got.astype(BF16).reshape(16, 16, QW)
        send_all(msend.at[ch], mall.at[0, ch], m_send.at[ch], m_recv.at[ch])

    rr, cc = iota((1024, 256), 0), iota((1024, 256), 1)
    spread[...] = (
        cc == 32 * (rr // 128) + 16 * ((rr // 8) % 2) + 2 * ((rr // 16) % 8) + (rr // 4) % 2
    ).astype(F32).astype(BF16)
    occ_t[...] = gated(occ, 0).astype(BF16)

    @pl.loop(0, 4)
    def _(k):
        rows = pl.ds(pl.multiple_of(k * 256, 256), 256)
        t1 = jnp.dot(spread[rows, :], occ_t[...], preferred_element_type=F32).astype(BF16)
        for n in range(4):
            got = lax.dot_general(
                t1, spread[n * 256 : (n + 1) * 256, :], (((1,), (1,)), ((), ())), preferred_element_type=F32
            )
            wide[rows, n * 256 : (n + 1) * 256] = jnp.where(r % 4 == c % 4, got, 0.0).astype(BF16)

    for ch in range(2):
        wait_all(hrecv.at[ch], h_recv.at[ch])
        for piece in range(CW // QW):
            t = ch * 4 + piece * 2
            for k in range(4):
                rows = pl.ds(k * 256, 256)
                got = jnp.dot(
                    wide[rows, :],
                    hrecv[ch, :, :, pl.ds(piece * QW, QW)].reshape(1024, QW),
                    preferred_element_type=F32,
                )
                both_t[t // 4, pl.ds(t % 4, 2), :, :, :, rows] = got.T.astype(BF16).reshape(2, 4, 2, 16, 256)

    def reach(u, phase, off, src, dst):
        axis = ORDERS[u % 3][phase]
        pos = dict(me)
        pos[axis] = (me[axis] + off) % 4
        return pltpu.make_async_remote_copy(
            src_ref=src,
            dst_ref=dst,
            send_sem=r_send.at[u, phase, off - 1],
            recv_sem=r_recv.at[u, phase, off - 1],
            device_id=device(pos, core),
            device_id_type=MESH,
        )

    sent = []

    def group(u):
        return (0, 1, 0, 1)[u // 2], u // 4, u % 2

    def copies(u, phase):
        order = ORDERS[u % 3]
        d1 = left_after(DIMS, order[0])
        d2 = left_after(d1, order[1])
        res = []
        for off in (2, 1, 3):
            axis = order[phase]
            k = (me[axis] + off) % 4
            if phase == 0:
                src, dst = send_a.at[u, off - 1], recv_a.at[u, off - 1]
            elif phase == 1:
                src, dst = acc_a[u].at[pick(d1, axis, k)], recv_b[u].at[off - 1]
            else:
                src, dst = acc_b[u].at[pick(d2, axis, k)], recv_c.at[u, off - 1]
            res.append((off, k, reach(u, phase, off, src, dst)))
        return res

    def phase_a(u):
        whose, ch, piece = group(u)
        axis = ORDERS[u % 3][0]
        right = mall[whose, ch, :, :, pl.ds(piece * QW, QW)].reshape(1024, QW)
        for off, k, cp in copies(u, 0):
            left = both_t[pick(DIMS, axis, k)].reshape(256, 1024)
            send_a[u, off - 1] = jnp.dot(left, right, preferred_element_type=F32).astype(BF16)
            cp.start()
            sent.append(cp)
        left = both_t[pick(DIMS, axis, me[axis])].reshape(256, 1024)
        d1 = left_after(DIMS, axis)
        acc_a[u][...] = jnp.dot(left, right, preferred_element_type=F32).reshape(shape_of(d1) + (16, QW))

    def phase_b(u):
        order = ORDERS[u % 3]
        d1 = left_after(DIMS, order[0])
        for _, _, cp in copies(u, 0):
            cp.wait_recv()
        total = acc_a[u][...]
        for off in (1, 2, 3):
            total += recv_a[u, off - 1].astype(F32).reshape(total.shape)
        acc_a[u][...] = total
        for _, _, cp in copies(u, 1):
            cp.start()
            sent.append(cp)

    def phase_c(u):
        order = ORDERS[u % 3]
        d1 = left_after(DIMS, order[0])
        for _, _, cp in copies(u, 1):
            cp.wait_recv()
        total = acc_a[u][pick(d1, order[1], me[order[1]])]
        for off in (1, 2, 3):
            total += recv_b[u][off - 1].reshape(total.shape)
        acc_b[u][...] = total
        for _, _, cp in copies(u, 2):
            cp.start()
            sent.append(cp)

    def finish(u):
        order = ORDERS[u % 3]
        d2 = left_after(left_after(DIMS, order[0]), order[1])
        for _, _, cp in copies(u, 2):
            cp.wait_recv()
        total = acc_b[u][pick(d2, order[2], me[order[2]])]
        for off in (1, 2, 3):
            total += recv_c[u, off - 1]
        total = total * (1.0 / 256.0)
        whose, ch, piece = group(u)
        c_of = core if whose == 0 else 1 - core
        for t in range(2):
            out[:, tile(ch * 4 + piece * 2 + t, c_of)] = total[:, t * 128 : (t + 1) * 128]

    def swap(ch):
        return pltpu.make_async_remote_copy(
            src_ref=mall.at[0, ch],
            dst_ref=mall.at[1, ch],
            send_sem=p_send.at[ch],
            recv_sem=p_recv.at[ch],
            device_id=partner,
            device_id_type=MESH,
        )

    for s in range(NU + 3):
        if s < NU:
            if s % 4 == 0:
                wait_all(mall.at[0, s // 4], m_recv.at[s // 4])
                swap(s // 4).start()
            if s % 4 == 2:
                swap(s // 4).wait_recv()
            phase_a(s)
        if 0 <= s - 1 < NU:
            phase_b(s - 1)
        if 0 <= s - 2 < NU:
            phase_c(s - 2)
        if 0 <= s - 3 < NU:
            finish(s - 3)

    for ch in range(2):
        wait_all(hsend.at[ch], h_send.at[ch])
        wait_all(msend.at[ch], m_send.at[ch])
        swap(ch).wait_send()
    for cp in theirs:
        cp.wait_send()
    for cp in sent:
        cp.wait_send()


def local(integrals, occupied, virtual, pair_mask, green_mask):
    vmem = pltpu.VMEM
    dma = pltpu.SemaphoreType.DMA
    acc_a, acc_b, recv_b = [], [], []
    for u in range(NU):
        d1 = left_after(DIMS, ORDERS[u % 3][0])
        d2 = left_after(d1, ORDERS[u % 3][1])
        acc_a.append(vmem(shape_of(d1) + (16, QW), F32))
        acc_b.append(vmem(shape_of(d2) + (16, QW), F32))
        recv_b.append(vmem((3,) + shape_of(d2) + (16, QW), F32))
    scratch = [
        vmem((4, 256, 1024), BF16),
        vmem((8, 1024), F32),
        vmem((256, 256), BF16),
        vmem((256, 256), BF16),
        vmem((4, 256, CW), BF16),
        vmem((2, 64, 16, CW), BF16),
        vmem((2, 64, 16, CW), BF16),
        vmem((2, 64, 16, CW), BF16),
        vmem((2, 2, 64, 16, CW), BF16),
        vmem((1024, 256), BF16),
        vmem((256, 256), BF16),
        vmem((1024, 1024), BF16),
        vmem((2, 4, 4, 2, 16, 1024), BF16),
        vmem((NU, 3, 256, QW), BF16),
        vmem((NU, 3, 256, QW), BF16),
        vmem((NU, 3, 16, QW), F32),
        *acc_a,
        *acc_b,
        *recv_b,
        dma((2, 4)), dma((2, 4)), dma((2, 4)),
        dma((2,)), dma((2,)), dma((2,)), dma((2,)), dma((2,)), dma((2,)),
        dma((NU, 3, 3)), dma((NU, 3, 3)),
    ]
    return pl.pallas_call(
        kernel,
        out_shape=jax.ShapeDtypeStruct((16, 2048), F32),
        in_specs=[
            pl.BlockSpec(memory_space=pl.ANY),
            pl.BlockSpec(memory_space=pltpu.VMEM),
            pl.BlockSpec(memory_space=pltpu.VMEM),
            pl.BlockSpec(memory_space=pltpu.SMEM),
            pl.BlockSpec(memory_space=pltpu.SMEM),
        ],
        out_specs=pl.BlockSpec(memory_space=pltpu.VMEM),
        scratch_shapes=scratch,
        compiler_params=pltpu.CompilerParams(
            collective_id=0, has_side_effects=True, vmem_limit_bytes=50 * 2**20
        ),
        name="polarizability",
    )(integrals.reshape(2, 256, 2048), occupied, virtual, pair_mask, green_mask)


def solution(mesh):
    return jax.shard_map(
        local,
        mesh=mesh,
        in_specs=(P(("row", "col"), None), P(), P(), P(), P()),
        out_specs=P(("row", "col"), None),
        check_vma=False,
    )
```

```python
import functools

import jax
import jax.numpy as jnp
from jax import lax
from jax.experimental import pallas as pl
from jax.experimental.pallas import tpu as pltpu
from jax.sharding import PartitionSpec as P

F32 = jnp.float32
BF16 = jnp.bfloat16
MESH = pl.DeviceIdType.MESH
CW = 512
QW = 256
NU = 8
LAGS = (8, 16, 24)
DIMS = ("ylo", "x", "z", "yhi")
SIZE = {"ylo": 2, "x": 4, "z": 4, "yhi": 2}
ORDERS = (("x", "y", "z"), ("y", "z", "x"), ("z", "x", "y"))


def parts_of(axis):
    return ("ylo", "yhi") if axis == "y" else (axis,)


def left_after(dims, axis):
    return tuple(d for d in dims if d not in parts_of(axis))


def pick(dims, axis, k):
    at = {"x": k, "z": k} if axis != "y" else {"ylo": k % 2, "yhi": k // 2}
    return tuple(at[d] if d in parts_of(axis) else slice(None) for d in dims)


def shape_of(dims):
    return tuple(SIZE[d] for d in dims)


def device(pos, core):
    return ((pos["y"] % 2) * 8 + pos["x"] * 2 + core, pos["z"] * 2 + pos["y"] // 2)


def iota(shape, axis):
    return lax.broadcasted_iota(jnp.int32, shape, axis)


def kernel(
    ints, occ_in, virt_in, pair_in, green_in, out,
    occ, virt, pair_gate, green_gate, mx, gate, vt, perm, hd, hsend, msend, hrecv, mall, spread, occ_t, wide, both_t,
    send_a, recv_a, recv_c, *rest,
):
    acc_a, acc_b, recv_b = rest[:NU], rest[NU : 2 * NU], rest[2 * NU : 3 * NU]
    x_own, x_send, x_recv, h_send, h_recv, m_send, m_recv, p_send, p_recv, r_send, r_recv, s_in, ready = rest[3 * NU :]
    row, col = lax.axis_index("row"), lax.axis_index("col")
    core = row % 2
    me = {"x": (row // 2) % 4, "y": (col % 2) * 2 + row // 8, "z": col // 2}
    chip = (row // 2) * 8 + col
    partner = (row - core + (1 - core), col)

    def other(i):
        pos = {
            "x": (me["x"] + i) % 4,
            "y": (me["y"] + i + i // 4) % 4,
            "z": (me["z"] + i + i // 16) % 4,
        }
        return pos

    def chip_of(pos):
        return ((pos["y"] % 2) * 4 + pos["x"]) * 8 + pos["z"] * 2 + pos["y"] // 2

    def along(axis, off):
        pos = dict(me)
        pos[axis] = (me[axis] + off) % 4
        return pos

    barrier = pltpu.get_barrier_semaphore()
    pl.semaphore_signal(barrier, inc=1, device_id=partner, device_id_type=MESH)
    for axis in ("x", "y", "z"):
        for off in (1, 2, 3):
            pl.semaphore_signal(
                barrier, inc=1, device_id=device(along(axis, off), core), device_id_type=MESH
            )
    small = []
    for n, (src, dst) in enumerate(((pair_in, pair_gate), (green_in, green_gate), (virt_in, virt), (occ_in, occ))):
        cp = pltpu.make_async_copy(src, dst, s_in.at[n])
        cp.start()
        small.append(cp)

    def tile(t, c):
        return pl.ds(pl.multiple_of((2 * t + c) * 128, 128), 128)

    own = []
    for ch in range(2):
        for t in range(4):
            cp = pltpu.make_async_copy(
                ints.at[:, :, tile(4 * ch + t, core)],
                mx.at[pl.ds(2 * core, 2), :, pl.ds(ch * CW + t * 128, 128)],
                x_own.at[ch, t],
            )
            cp.start()
            own.append(cp)

    pl.semaphore_wait(barrier, 10)
    theirs = []
    for ch in range(2):
        for t in range(4):
            cp = pltpu.make_async_remote_copy(
                src_ref=ints.at[:, :, tile(4 * ch + t, 1 - core)],
                dst_ref=mx.at[pl.ds(2 * core, 2), :, pl.ds(ch * CW + t * 128, 128)],
                send_sem=x_send.at[ch, t],
                recv_sem=x_recv.at[ch, t],
                device_id=partner,
                device_id_type=MESH,
            )
            cp.start()
            theirs.append(cp)

    def hop(n, axis):
        for off in (1, 2, 3):
            pl.semaphore_signal(
                ready.at[n], inc=1, device_id=device(along(axis, off), core), device_id_type=MESH
            )

    hop(0, "y")
    for cp in small:
        cp.wait()
    lane = iota((1, 128), 1)
    for g in range(4):
        for t in range(8):
            a = pair_gate[(row // 4) * 4 + g, 4 * t + 2 * core].astype(F32)
            b = pair_gate[(row // 4) * 4 + g, 4 * t + 2 * core + 1].astype(F32)
            gate[g : g + 1, t * 128 : (t + 1) * 128] = jnp.where(lane < 64, a, b)
    lane = iota((1, 256), 1)

    def gated(ref, which):
        blocks = []
        for a in range(4):
            line = jnp.zeros((1, 256), F32)
            for b in range(4):
                line = jnp.where(lane // 64 == b, green_gate[which, a, b].astype(F32), line)
            blocks.append(ref[64 * a : 64 * a + 64, :].astype(F32) * line)
        return jnp.concatenate(blocks, axis=0)

    vt[...] = gated(virt, 1).T.astype(BF16)
    r, c = iota((256, 256), 0), iota((256, 256), 1)
    perm[...] = (c == ((r // 4) % 4) * 64 + (r // 16) * 4 + r % 4).astype(F32).astype(BF16)

    pl.semaphore_wait(ready.at[0], 3)
    hop(1, "z")

    def send_all(src, dst, send_sem, recv_sem):
        @pl.loop(1, 64)
        def _(i):
            pos = other(i)
            pltpu.make_async_remote_copy(
                src_ref=src.at[chip_of(pos)],
                dst_ref=dst.at[chip],
                send_sem=send_sem,
                recv_sem=recv_sem,
                device_id=device(pos, core),
                device_id_type=MESH,
            ).start()

        dst[chip] = src[chip]

    def wait_all(ref, sem):
        pltpu.make_async_copy(ref.at[pl.ds(0, 63)], ref.at[pl.ds(0, 63)], sem).wait()

    for ch in range(2):
        for t in range(4):
            own[4 * ch + t].wait()
            theirs[4 * ch + t].wait_recv()
        for piece in range(CW // QW):
            lanes = pl.ds(ch * CW + piece * QW, QW)
            part = pl.ds(piece * QW, QW)

            @pl.loop(0, 4)
            def _(k):
                for g in range(4):
                    rows = pl.ds(64 * g, 64)
                    mx[k, rows, lanes] = (mx[k, rows, lanes].astype(F32) * gate[g : g + 1, lanes]).astype(BF16)
                hd[k, :, part] = jnp.dot(vt[...], mx[k, :, lanes], preferred_element_type=F32).astype(BF16)

            for g in range(4):
                rows = pl.ds(64 * g, 64)
                got = jnp.dot(perm[...], hd[:, rows, part].reshape(256, QW), preferred_element_type=F32)
                hsend[ch, pl.ds(16 * g, 16), :, part] = got.astype(BF16).reshape(16, 16, QW)
        if ch == 0:
            pl.semaphore_wait(ready.at[1], 3)
        send_all(hsend.at[ch], hrecv.at[ch], h_send.at[ch], h_recv.at[ch])
    for ch in range(2):
        for piece in range(CW // QW):
            lanes = pl.ds(ch * CW + piece * QW, QW)
            part = pl.ds(piece * QW, QW)
            for g in range(4):
                rows = pl.ds(64 * g, 64)
                got = jnp.dot(perm[...], mx[:, rows, lanes].reshape(256, QW), preferred_element_type=F32)
                msend[ch, pl.ds(16 * g, 16), :, part] = got.astype(BF16).reshape(16, 16, QW)
        send_all(msend.at[ch], mall.at[0, ch], m_send.at[ch], m_recv.at[ch])

    rr, cc = iota((1024, 256), 0), iota((1024, 256), 1)
    spread[...] = (
        cc == 32 * (rr // 128) + 16 * ((rr // 8) % 2) + 2 * ((rr // 16) % 8) + (rr // 4) % 2
    ).astype(F32).astype(BF16)
    occ_t[...] = gated(occ, 0).astype(BF16)

    @pl.loop(0, 4)
    def _(k):
        rows = pl.ds(pl.multiple_of(k * 256, 256), 256)
        t1 = jnp.dot(spread[rows, :], occ_t[...], preferred_element_type=F32).astype(BF16)
        for n in range(4):
            got = lax.dot_general(
                t1, spread[n * 256 : (n + 1) * 256, :], (((1,), (1,)), ((), ())), preferred_element_type=F32
            )
            wide[rows, n * 256 : (n + 1) * 256] = jnp.where(r % 4 == c % 4, got, 0.0).astype(BF16)

    for ch in range(2):
        wait_all(hrecv.at[ch], h_recv.at[ch])
        for piece in range(CW // QW):
            t = ch * 4 + piece * 2
            for k in range(4):
                rows = pl.ds(k * 256, 256)
                got = jnp.dot(
                    wide[rows, :],
                    hrecv[ch, :, :, pl.ds(piece * QW, QW)].reshape(1024, QW),
                    preferred_element_type=F32,
                )
                both_t[t // 4, pl.ds(t % 4, 2), :, :, :, rows] = got.T.astype(BF16).reshape(2, 4, 2, 16, 256)

    def reach(u, phase, off, src, dst):
        axis = ORDERS[u % 3][phase]
        pos = along(axis, off)
        return pltpu.make_async_remote_copy(
            src_ref=src,
            dst_ref=dst,
            send_sem=r_send.at[u, phase, off - 1],
            recv_sem=r_recv.at[u, phase, off - 1],
            device_id=device(pos, core),
            device_id_type=MESH,
        )

    sent = []

    def group(u):
        return (0, 1, 0, 1)[u // 2], u // 4, u % 2

    def copies(u, phase):
        order = ORDERS[u % 3]
        d1 = left_after(DIMS, order[0])
        d2 = left_after(d1, order[1])
        res = []
        for off in (2, 1, 3):
            axis = order[phase]
            k = (me[axis] + off) % 4
            if phase == 0:
                src, dst = send_a.at[u, off - 1], recv_a.at[u, off - 1]
            elif phase == 1:
                src, dst = acc_a[u].at[pick(d1, axis, k)], recv_b[u].at[off - 1]
            else:
                src, dst = acc_b[u].at[pick(d2, axis, k)], recv_c.at[u, off - 1]
            res.append((off, k, reach(u, phase, off, src, dst)))
        return res

    def phase_a(u):
        whose, ch, piece = group(u)
        axis = ORDERS[u % 3][0]
        right = mall[whose, ch, :, :, pl.ds(piece * QW, QW)].reshape(1024, QW)
        for off, k, cp in copies(u, 0):
            left = both_t[pick(DIMS, axis, k)].reshape(256, 1024)
            send_a[u, off - 1] = jnp.dot(left, right, preferred_element_type=F32).astype(BF16)
            cp.start()
            sent.append(cp)
        left = both_t[pick(DIMS, axis, me[axis])].reshape(256, 1024)
        d1 = left_after(DIMS, axis)
        acc_a[u][...] = jnp.dot(left, right, preferred_element_type=F32).reshape(shape_of(d1) + (16, QW))

    def phase_b(u):
        order = ORDERS[u % 3]
        d1 = left_after(DIMS, order[0])
        for _, _, cp in copies(u, 0):
            cp.wait_recv()
        total = acc_a[u][...]
        for off in (1, 2, 3):
            total += recv_a[u, off - 1].astype(F32).reshape(total.shape)
        acc_a[u][...] = total
        for _, _, cp in copies(u, 1):
            cp.start()
            sent.append(cp)

    def phase_c(u):
        order = ORDERS[u % 3]
        d1 = left_after(DIMS, order[0])
        for _, _, cp in copies(u, 1):
            cp.wait_recv()
        total = acc_a[u][pick(d1, order[1], me[order[1]])]
        for off in (1, 2, 3):
            total += recv_b[u][off - 1].reshape(total.shape)
        acc_b[u][...] = total
        for _, _, cp in copies(u, 2):
            cp.start()
            sent.append(cp)

    def finish(u):
        order = ORDERS[u % 3]
        d2 = left_after(left_after(DIMS, order[0]), order[1])
        for _, _, cp in copies(u, 2):
            cp.wait_recv()
        total = acc_b[u][pick(d2, order[2], me[order[2]])]
        for off in (1, 2, 3):
            total += recv_c[u, off - 1]
        total = total * (1.0 / 256.0)
        whose, ch, piece = group(u)
        c_of = core if whose == 0 else 1 - core
        for t in range(2):
            out[:, tile(ch * 4 + piece * 2 + t, c_of)] = total[:, t * 128 : (t + 1) * 128]

    def swap(ch):
        return pltpu.make_async_remote_copy(
            src_ref=mall.at[0, ch],
            dst_ref=mall.at[1, ch],
            send_sem=p_send.at[ch],
            recv_sem=p_recv.at[ch],
            device_id=partner,
            device_id_type=MESH,
        )

    for s in range(NU + LAGS[2]):
        if s < NU:
            if s % 4 == 0:
                wait_all(mall.at[0, s // 4], m_recv.at[s // 4])
                swap(s // 4).start()
            if s % 4 == 2:
                swap(s // 4).wait_recv()
            phase_a(s)
        if 0 <= s - LAGS[0] < NU:
            phase_b(s - LAGS[0])
        if 0 <= s - LAGS[1] < NU:
            phase_c(s - LAGS[1])
        if 0 <= s - LAGS[2] < NU:
            finish(s - LAGS[2])

    for ch in range(2):
        wait_all(hsend.at[ch], h_send.at[ch])
        wait_all(msend.at[ch], m_send.at[ch])
        swap(ch).wait_send()
    for cp in theirs:
        cp.wait_send()
    for cp in sent:
        cp.wait_send()


def local(integrals, occupied, virtual, pair_mask, green_mask):
    vmem = pltpu.VMEM
    dma = pltpu.SemaphoreType.DMA
    acc_a, acc_b, recv_b = [], [], []
    for u in range(NU):
        d1 = left_after(DIMS, ORDERS[u % 3][0])
        d2 = left_after(d1, ORDERS[u % 3][1])
        acc_a.append(vmem(shape_of(d1) + (16, QW), F32))
        acc_b.append(vmem(shape_of(d2) + (16, QW), F32))
        recv_b.append(vmem((3,) + shape_of(d2) + (16, QW), F32))
    scratch = [
        vmem((256, 256), BF16),
        vmem((256, 256), BF16),
        pltpu.SMEM((16, 32), jnp.int32),
        pltpu.SMEM((2, 4, 4), jnp.int32),
        vmem((4, 256, 1024), BF16),
        vmem((8, 1024), F32),
        vmem((256, 256), BF16),
        vmem((256, 256), BF16),
        vmem((4, 256, CW), BF16),
        vmem((2, 64, 16, CW), BF16),
        vmem((2, 64, 16, CW), BF16),
        vmem((2, 64, 16, CW), BF16),
        vmem((2, 2, 64, 16, CW), BF16),
        vmem((1024, 256), BF16),
        vmem((256, 256), BF16),
        vmem((1024, 1024), BF16),
        vmem((2, 4, 4, 2, 16, 1024), BF16),
        vmem((NU, 3, 256, QW), BF16),
        vmem((NU, 3, 256, QW), BF16),
        vmem((NU, 3, 16, QW), F32),
        *acc_a,
        *acc_b,
        *recv_b,
        dma((2, 4)), dma((2, 4)), dma((2, 4)),
        dma((2,)), dma((2,)), dma((2,)), dma((2,)), dma((2,)), dma((2,)),
        dma((NU, 3, 3)), dma((NU, 3, 3)), dma((4,)),
        pltpu.SemaphoreType.REGULAR((2,)),
    ]
    return pl.pallas_call(
        kernel,
        out_shape=jax.ShapeDtypeStruct((16, 2048), F32),
        in_specs=[
            pl.BlockSpec(memory_space=pltpu.HBM),
            pl.BlockSpec(memory_space=pltpu.HBM),
            pl.BlockSpec(memory_space=pltpu.HBM),
            pl.BlockSpec(memory_space=pltpu.HBM),
            pl.BlockSpec(memory_space=pltpu.HBM),
        ],
        out_specs=pl.BlockSpec(memory_space=pltpu.VMEM),
        scratch_shapes=scratch,
        compiler_params=pltpu.CompilerParams(
            collective_id=0, has_side_effects=True, vmem_limit_bytes=61 * 2**20
        ),
        name="polarizability",
    )(integrals.reshape(2, 256, 2048), occupied, virtual, pair_mask, green_mask)


def solution(mesh):
    return jax.shard_map(
        local,
        mesh=mesh,
        in_specs=(P(("row", "col"), None), P(), P(), P(), P()),
        out_specs=P(("row", "col"), None),
        check_vma=False,
    )
```

```python
import functools

import jax
import jax.numpy as jnp
from jax import lax
from jax.experimental import pallas as pl
from jax.experimental.pallas import tpu as pltpu
from jax.sharding import PartitionSpec as P

F32 = jnp.float32
BF16 = jnp.bfloat16
MESH = pl.DeviceIdType.MESH
QW = 256
H_CHUNKS = ((0, 512), (512, 512))
M_CHUNKS = ((0, 512), (512, 256), (768, 256))
UNITS = tuple(
    (ch, whose, piece) for ch, (_, w) in enumerate(M_CHUNKS) for whose in range(2) for piece in range(w // QW)
)
NT = 2 * len(UNITS)
DIMS = ("ylo", "x", "z", "yhi")
SIZE = {"ylo": 2, "x": 4, "z": 4, "yhi": 2}
ORDERS = (("x", "y", "z"), ("y", "z", "x"), ("z", "x", "y"))


def parts_of(axis):
    return ("ylo", "yhi") if axis == "y" else (axis,)


def left_after(dims, axis):
    return tuple(d for d in dims if d not in parts_of(axis))


def pick(dims, axis, k):
    at = {"x": k, "z": k} if axis != "y" else {"ylo": k % 2, "yhi": k // 2}
    return tuple(at[d] if d in parts_of(axis) else slice(None) for d in dims)


def shape_of(dims):
    return tuple(SIZE[d] for d in dims)


def device(pos, core):
    return ((pos["y"] % 2) * 8 + pos["x"] * 2 + core, pos["z"] * 2 + pos["y"] // 2)


def iota(shape, axis):
    return lax.broadcasted_iota(jnp.int32, shape, axis)


def order_of(t):
    return ORDERS[t % 3]


def dims_of(t):
    d1 = left_after(DIMS, order_of(t)[0])
    return d1, left_after(d1, order_of(t)[1])


AHEAD = len(M_CHUNKS)
PLAN = (("a", 0, 8), ("b", 0, 8), ("c", 0, 8), ("f", 0, 8))


def kernel(*refs):
    refs = list(refs)

    def take(n):
        got = refs[:n]
        del refs[:n]
        return got

    ints, occ_in, virt_in, pair_in, green_in, out = take(6)
    occ, virt, pair_gate, green_gate = take(4)
    mx, gate, vt, perm, hd, spread, occ_t, wide, both_t, stage = take(10)
    hsend, hrecv = take(len(H_CHUNKS)), take(len(H_CHUNKS))
    msend, mall = take(len(M_CHUNKS)), take(len(M_CHUNKS))
    (send_a,) = take(1)
    recv_a, acc_a, send_b, recv_b, acc_b, send_c, recv_c = (take(NT) for _ in range(7))
    x_own, x_send, x_recv, h_send, h_recv, m_send, m_recv, p_send, p_recv, r_send, r_recv, s_in, ready = refs
    row, col = lax.axis_index("row"), lax.axis_index("col")
    core = row % 2
    me = {"x": (row // 2) % 4, "y": (col % 2) * 2 + row // 8, "z": col // 2}
    chip = (row // 2) * 8 + col
    partner = (row - core + (1 - core), col)

    def along(axis, off):
        pos = dict(me)
        pos[axis] = (me[axis] + off) % 4
        return pos

    def other(i):
        return {
            "x": (me["x"] + i) % 4,
            "y": (me["y"] + i + i // 4) % 4,
            "z": (me["z"] + i + i // 16) % 4,
        }

    def chip_of(pos):
        return ((pos["y"] % 2) * 4 + pos["x"]) * 8 + pos["z"] * 2 + pos["y"] // 2

    barrier = pltpu.get_barrier_semaphore()
    pl.semaphore_signal(barrier, inc=1, device_id=partner, device_id_type=MESH)
    lines = [device(along(axis, off), core) for off in (2, 1, 3) for axis in ("x", "y", "z")]
    for there in lines:
        pl.semaphore_signal(barrier, inc=1, device_id=there, device_id_type=MESH)

    small = []
    for n, (src, dst) in enumerate(((pair_in, pair_gate), (green_in, green_gate), (virt_in, virt), (occ_in, occ))):
        cp = pltpu.make_async_copy(src, dst, s_in.at[n])
        cp.start()
        small.append(cp)

    def tile(t, c):
        return pl.ds(pl.multiple_of((2 * t + c) * 128, 128), 128)

    mine = mx.at[pl.ds(2 * core, 2)]
    for t in range(8):
        pltpu.make_async_copy(ints.at[:, :, tile(t, core)], mine.at[:, :, pl.ds(t * 128, 128)], x_own).start()

    r, c = iota((256, 256), 0), iota((256, 256), 1)
    perm[...] = (c == ((r // 4) % 4) * 64 + (r // 16) * 4 + r % 4).astype(F32).astype(BF16)
    lane = iota((1, 128), 1)
    small[0].wait()
    for g in range(4):
        for t in range(8):
            a = pair_gate[(row // 4) * 4 + g, 4 * t + 2 * core].astype(F32)
            b = pair_gate[(row // 4) * 4 + g, 4 * t + 2 * core + 1].astype(F32)
            gate[g : g + 1, t * 128 : (t + 1) * 128] = jnp.where(lane < 64, a, b)

    def gated(ref, which):
        lane = iota((1, 256), 1)
        blocks = []
        for a in range(4):
            line = jnp.zeros((1, 256), F32)
            for b in range(4):
                line = jnp.where(lane // 64 == b, green_gate[which, a, b].astype(F32), line)
            blocks.append(ref[64 * a : 64 * a + 64, :].astype(F32) * line)
        return jnp.concatenate(blocks, axis=0)

    small[1].wait()
    small[2].wait()
    vt[...] = gated(virt, 1).T.astype(BF16)

    pl.semaphore_wait(barrier, 10)
    for there in lines:
        pl.semaphore_signal(ready.at[0], inc=1, device_id=there, device_id_type=MESH)
    for t in range(8):
        pltpu.make_async_remote_copy(
            src_ref=ints.at[:, :, tile(t, 1 - core)],
            dst_ref=mine.at[:, :, pl.ds(t * 128, 128)],
            send_sem=x_send,
            recv_sem=x_recv.at[t // 2],
            device_id=partner,
            device_id_type=MESH,
        ).start()

    def wait_for(ref, sem):
        pltpu.make_async_copy(ref, ref, sem).wait()

    def half(first, lanes):
        @pl.loop(0, 2)
        def _(n):
            k = first + n
            for g in range(4):
                rows = pl.ds(64 * g, 64)
                mx[k, rows, lanes] = (mx[k, rows, lanes].astype(F32) * gate[g : g + 1, lanes]).astype(BF16)
            hd[k, :, lanes] = jnp.dot(vt[...], mx[k, :, lanes], preferred_element_type=F32).astype(BF16)

    def pieces(start, width):
        return [(start + n, n) for n in range(0, width, QW)]

    def to_chips(src, dst, lanes, part):
        for g in range(4):
            got = jnp.dot(
                perm[...], src[:, pl.ds(64 * g, 64), lanes].reshape(256, QW), preferred_element_type=F32
            )
            dst[pl.ds(16 * g, 16), :, part] = got.astype(BF16).reshape(16, 16, QW)

    def send_all(src, dst, send_sem, recv_sem, only=None):
        @pl.loop(1, 64)
        def _(i):
            pos = other(i)

            def start():
                pltpu.make_async_remote_copy(
                    src_ref=src.at[chip_of(pos)],
                    dst_ref=dst.at[chip],
                    send_sem=send_sem,
                    recv_sem=recv_sem,
                    device_id=device(pos, core),
                    device_id_type=MESH,
                ).start()

            if only is None:
                start()
            else:
                apart = (i % 4) * ((i + i // 4) % 4) * ((i + i // 16) % 4)
                pl.when((apart == 0) if only == 0 else (apart != 0))(start)

    def send_h(n, only=None):
        send_all(hsend[n], hrecv[n], h_send.at[n], h_recv.at[n], only)
        if only != 1:
            hrecv[n][chip] = hsend[n][chip]

    def send_m(n):
        send_all(msend[n], mall[n].at[0], m_send.at[n], m_recv.at[n])
        mall[n][0, chip] = msend[n][chip]

    def wait_all(ref, sem):
        wait_for(ref.at[pl.ds(0, 63)], sem)

    wait_for(mine, x_own)
    for start, _ in pieces(0, 1024):
        half(2 * core, pl.ds(start, QW))

    def make_h(n):
        first, width = H_CHUNKS[n]
        for start, at in pieces(first, width):
            wait_for(mx.at[pl.ds(2 - 2 * core, 2), :, pl.ds(start, QW)], x_recv.at[start // QW])
            half(2 - 2 * core, pl.ds(start, QW))
            to_chips(hd, hsend[n], pl.ds(start, QW), pl.ds(at, QW))

    def make_m(n):
        first, width = M_CHUNKS[n]
        for start, at in pieces(first, width):
            to_chips(mx, msend[n], pl.ds(start, QW), pl.ds(at, QW))

    pl.semaphore_wait(ready.at[0], 9)
    for off in (1, 2, 3):
        there = device(along("z", off), core)
        pl.semaphore_signal(ready.at[1], inc=1, device_id=there, device_id_type=MESH)
    make_h(0)
    send_h(0, 0)
    make_h(1)
    pl.semaphore_wait(ready.at[1], 3)
    send_h(0, 1)
    send_h(1)
    for n in range(2, len(H_CHUNKS)):
        make_h(n)
        send_h(n)
    for n in range(len(M_CHUNKS)):
        make_m(n)
        if n < AHEAD:
            send_m(n)

    rr, cc = iota((1024, 256), 0), iota((1024, 256), 1)
    spread[...] = (
        cc == 32 * (rr // 128) + 16 * ((rr // 8) % 2) + 2 * ((rr // 16) % 8) + (rr // 4) % 2
    ).astype(F32).astype(BF16)
    small[3].wait()
    occ_t[...] = gated(occ, 0).astype(BF16)

    @pl.loop(0, 4)
    def _(k):
        rows = pl.ds(pl.multiple_of(k * 256, 256), 256)
        t1 = jnp.dot(spread[rows, :], occ_t[...], preferred_element_type=F32).astype(BF16)
        for n in range(4):
            got = lax.dot_general(
                t1, spread[n * 256 : (n + 1) * 256, :], (((1,), (1,)), ((), ())), preferred_element_type=F32
            )
            wide[rows, n * 256 : (n + 1) * 256] = jnp.where(r % 4 == c % 4, got, 0.0).astype(BF16)

    for n, (first, width) in enumerate(H_CHUNKS):
        wait_all(hrecv[n], h_recv.at[n])
        if n == len(H_CHUNKS) - 1 and AHEAD < len(M_CHUNKS):
            send_m(AHEAD)
        for start, at in pieces(first, width):
            t = start // 128
            for k in range(4):
                rows = pl.ds(k * 256, 256)
                got = jnp.dot(
                    wide[rows, :], hrecv[n][:, :, pl.ds(at, QW)].reshape(1024, QW), preferred_element_type=F32
                )
                both_t[t // 4, pl.ds(t % 4, 2), :, :, :, rows] = got.T.astype(BF16).reshape(2, 4, 2, 16, 256)

    def copies(t, phase):
        order = order_of(t)
        d1, d2 = dims_of(t)
        axis = order[phase]
        res = []
        for off in (2, 1, 3):
            k = (me[axis] + off) % 4
            if phase == 0:
                src = send_a.at[(t // 2,) + pick(DIMS, axis, k) + (slice(None), pl.ds((t % 2) * 128, 128))]
                dst = recv_a[t].at[off - 1]
            elif phase == 1:
                src, dst = send_b[t].at[pick(d1, axis, k)], recv_b[t].at[off - 1]
            else:
                src, dst = send_c[t].at[pick(d2, axis, k)], recv_c[t].at[off - 1]
            res.append(
                pltpu.make_async_remote_copy(
                    src_ref=src,
                    dst_ref=dst,
                    send_sem=r_send.at[phase],
                    recv_sem=r_recv.at[t, phase],
                    device_id=device(along(axis, off), core),
                    device_id_type=MESH,
                )
            )
        return res

    def launch(t, phase):
        for cp in copies(t, phase):
            cp.start()

    def phase_a(u):
        ch, whose, piece = UNITS[u]
        right = mall[ch][whose, :, :, pl.ds(piece * QW, QW)].reshape(1024, QW)
        for ylo in range(2):
            for x in (0, 2):
                left = both_t[ylo, x : x + 2].reshape(256, 1024)
                got = jnp.dot(left, right, preferred_element_type=F32).reshape(2, 4, 2, 16, QW)
                stage[ylo, x : x + 2] = got
                send_a[u, ylo, x : x + 2] = got.astype(BF16)
        for t in (2 * u, 2 * u + 1):
            launch(t, 0)
            axis = order_of(t)[0]
            acc_a[t][...] = stage[pick(DIMS, axis, me[axis]) + (slice(None), pl.ds((t % 2) * 128, 128))]

    def phase_b(t):
        wait_for(recv_a[t], r_recv.at[t, 0])
        total = acc_a[t][...]
        for off in (1, 2, 3):
            total += recv_a[t][off - 1].astype(F32)
        acc_a[t][...] = total
        send_b[t][...] = total.astype(send_b[t].dtype)
        launch(t, 1)

    def phase_c(t):
        axis = order_of(t)[1]
        wait_for(recv_b[t], r_recv.at[t, 1])
        total = acc_a[t][pick(dims_of(t)[0], axis, me[axis])]
        for off in (1, 2, 3):
            total += recv_b[t][off - 1].astype(F32)
        acc_b[t][...] = total
        send_c[t][...] = total.astype(BF16)
        launch(t, 2)

    def finish(t):
        axis = order_of(t)[2]
        wait_for(recv_c[t], r_recv.at[t, 2])
        total = acc_b[t][pick(dims_of(t)[1], axis, me[axis])]
        for off in (1, 2, 3):
            total += recv_c[t][off - 1].astype(F32)
        ch, whose, piece = UNITS[t // 2]
        at = (M_CHUNKS[ch][0] + piece * QW) // 128 + t % 2
        out[:, tile(at, core if whose == 0 else 1 - core)] = total * (1.0 / 256.0)

    def swap(ch):
        return pltpu.make_async_remote_copy(
            src_ref=mall[ch].at[0],
            dst_ref=mall[ch].at[1],
            send_sem=p_send.at[ch],
            recv_sem=p_recv.at[ch],
            device_id=partner,
            device_id_type=MESH,
        )

    for name, u in [(name, u) for name, first, last in PLAN for u in range(first, last)]:
        if name == "a":
            ch, whose, piece = UNITS[u]
            if piece == 0 and whose == 0:
                wait_all(mall[ch].at[0], m_recv.at[ch])
                if ch + AHEAD + 1 < len(M_CHUNKS):
                    send_m(ch + AHEAD + 1)
                swap(ch).start()
            if piece == 0 and whose == 1:
                swap(ch).wait_recv()
            phase_a(u)
        else:
            for t in (2 * u, 2 * u + 1):
                {"b": phase_b, "c": phase_c, "f": finish}[name](t)

    for n in range(len(H_CHUNKS)):
        wait_all(hsend[n], h_send.at[n])
    for n in range(len(M_CHUNKS)):
        wait_all(msend[n], m_send.at[n])
        swap(n).wait_send()
    wait_for(mine, x_send)
    wait_for(send_a.at[pl.ds(0, NT * 3 // 8)], r_send.at[0])
    wait_for(mx.at[pl.ds(0, 3), pl.ds(0, NT * 8)], r_send.at[1])
    wait_for(mx.at[pl.ds(0, 3), pl.ds(0, NT * 2)], r_send.at[2])


def local(integrals, occupied, virtual, pair_mask, green_mask):
    vmem = pltpu.VMEM
    dma = pltpu.SemaphoreType.DMA
    nh, nm = len(H_CHUNKS), len(M_CHUNKS)
    whole = shape_of(DIMS)
    d1 = [shape_of(dims_of(t)[0]) + (16, 128) for t in range(NT)]
    d2 = [shape_of(dims_of(t)[1]) + (16, 128) for t in range(NT)]
    scratch = [
        vmem((256, 256), BF16),
        vmem((256, 256), BF16),
        pltpu.SMEM((16, 32), jnp.int32),
        pltpu.SMEM((2, 4, 4), jnp.int32),
        vmem((4, 256, 1024), BF16),
        vmem((8, 1024), F32),
        vmem((256, 256), BF16),
        vmem((256, 256), BF16),
        vmem((4, 256, 1024), BF16),
        vmem((1024, 256), BF16),
        vmem((256, 256), BF16),
        vmem((1024, 1024), BF16),
        vmem(whole + (16, 1024), BF16),
        vmem(whole + (16, QW), F32),
        *[vmem((64, 16, w), BF16) for _, w in H_CHUNKS],
        *[vmem((64, 16, w), BF16) for _, w in H_CHUNKS],
        *[vmem((64, 16, w), BF16) for _, w in M_CHUNKS],
        *[vmem((2, 64, 16, w), BF16) for _, w in M_CHUNKS],
        vmem((len(UNITS),) + whole + (16, QW), BF16),
        *[vmem((3,) + s, BF16) for s in d1],
        *[vmem(s, F32) for s in d1],
        *[vmem(s, BF16) for s in d1],
        *[vmem((3,) + s, BF16) for s in d2],
        *[vmem(s, F32) for s in d2],
        *[vmem(s, BF16) for s in d2],
        *[vmem((3, 16, 128), BF16) for _ in d2],
        dma, dma, dma((4,)),
        dma((nh,)), dma((nh,)), dma((nm,)), dma((nm,)), dma((nm,)), dma((nm,)),
        dma((3,)), dma((NT, 3)), dma((4,)),
        pltpu.SemaphoreType.REGULAR((2,)),
    ]
    return pl.pallas_call(
        kernel,
        out_shape=jax.ShapeDtypeStruct((16, 2048), F32),
        in_specs=[pl.BlockSpec(memory_space=pltpu.HBM)] * 5,
        out_specs=pl.BlockSpec(memory_space=pltpu.VMEM),
        scratch_shapes=scratch,
        compiler_params=pltpu.CompilerParams(
            collective_id=0, has_side_effects=True, vmem_limit_bytes=61 * 2**20
        ),
        name="polarizability",
    )(integrals.reshape(2, 256, 2048), occupied, virtual, pair_mask, green_mask)


def solution(mesh):
    return jax.shard_map(
        local,
        mesh=mesh,
        in_specs=(P(("row", "col"), None), P(), P(), P(), P()),
        out_specs=P(("row", "col"), None),
        check_vma=False,
    )
```

```python
import functools

import jax
import jax.numpy as jnp
from jax import lax
from jax.experimental import pallas as pl
from jax.experimental.pallas import tpu as pltpu
from jax.sharding import PartitionSpec as P

F32 = jnp.float32
BF16 = jnp.bfloat16
MESH = pl.DeviceIdType.MESH
QW = 256
H_CHUNKS = ((0, 256), (256, 256), (512, 512))
M_CHUNKS = ((0, 256), (256, 256), (512, 512))
UNITS = tuple(
    (ch, whose, piece) for ch, (_, w) in enumerate(M_CHUNKS) for whose in range(2) for piece in range(w // QW)
)
NT = 2 * len(UNITS)
DIMS = ("ylo", "x", "z", "yhi")
SIZE = {"ylo": 2, "x": 4, "z": 4, "yhi": 2}
ORDERS = (("x", "y", "z"), ("y", "z", "x"), ("z", "x", "y"))


def parts_of(axis):
    return ("ylo", "yhi") if axis == "y" else (axis,)


def left_after(dims, axis):
    return tuple(d for d in dims if d not in parts_of(axis))


def pick(dims, axis, k):
    at = {"x": k, "z": k} if axis != "y" else {"ylo": k % 2, "yhi": k // 2}
    return tuple(at[d] if d in parts_of(axis) else slice(None) for d in dims)


def shape_of(dims):
    return tuple(SIZE[d] for d in dims)


def device(pos, core):
    return ((pos["y"] % 2) * 8 + pos["x"] * 2 + core, pos["z"] * 2 + pos["y"] // 2)


def iota(shape, axis):
    return lax.broadcasted_iota(jnp.int32, shape, axis)


def order_of(t):
    return ORDERS[t % 3]


def dims_of(t):
    d1 = left_after(DIMS, order_of(t)[0])
    return d1, left_after(d1, order_of(t)[1])


DIRECT = (6, 7)
AHEAD = len(M_CHUNKS)
PLAN = (("a", 0, 8), ("b", 0, 8), ("c", 0, 8), ("f", 0, 8))


DIRECT_TILES = tuple(2 * u + n for u in DIRECT for n in range(2))


def kernel(*refs):
    refs = list(refs)

    def take(n):
        got = refs[:n]
        del refs[:n]
        return got

    ints, occ_in, virt_in, pair_in, green_in, out = take(6)
    occ, virt, pair_gate, green_gate = take(4)
    mx, gate, vt, perm, hd, spread, occ_t, wide, both_t, stage = take(10)
    hsend, hrecv = take(len(H_CHUNKS)), take(len(H_CHUNKS))
    msend, mall = take(len(M_CHUNKS)), take(len(M_CHUNKS))
    (send_a,) = take(1)
    recv_a, acc_a, send_b, recv_b, acc_b, send_c, recv_c = (take(NT) for _ in range(7))
    recv_d = dict(zip(DIRECT_TILES, take(len(DIRECT_TILES))))
    x_own, x_send, x_recv, h_send, h_recv, m_send, m_recv, p_send, p_recv, r_send, r_recv, s_in, ready = refs
    row, col = lax.axis_index("row"), lax.axis_index("col")
    core = row % 2
    me = {"x": (row // 2) % 4, "y": (col % 2) * 2 + row // 8, "z": col // 2}
    chip = (row // 2) * 8 + col
    partner = (row - core + (1 - core), col)

    def along(axis, off):
        pos = dict(me)
        pos[axis] = (me[axis] + off) % 4
        return pos

    def other(i):
        return {
            "x": (me["x"] + i) % 4,
            "y": (me["y"] + i + i // 4) % 4,
            "z": (me["z"] + i + i // 16) % 4,
        }

    def chip_of(pos):
        return ((pos["y"] % 2) * 4 + pos["x"]) * 8 + pos["z"] * 2 + pos["y"] // 2

    barrier = pltpu.get_barrier_semaphore()
    pl.semaphore_signal(barrier, inc=1, device_id=partner, device_id_type=MESH)
    lines = [device(along(axis, off), core) for off in (2, 1, 3) for axis in ("x", "y", "z")]
    for there in lines:
        pl.semaphore_signal(barrier, inc=1, device_id=there, device_id_type=MESH)

    small = []
    for n, (src, dst) in enumerate(((pair_in, pair_gate), (green_in, green_gate), (virt_in, virt), (occ_in, occ))):
        cp = pltpu.make_async_copy(src, dst, s_in.at[n])
        cp.start()
        small.append(cp)

    def tile(t, c):
        return pl.ds(pl.multiple_of((2 * t + c) * 128, 128), 128)

    mine = mx.at[pl.ds(2 * core, 2)]
    for t in range(8):
        pltpu.make_async_copy(ints.at[:, :, tile(t, core)], mine.at[:, :, pl.ds(t * 128, 128)], x_own).start()

    r, c = iota((256, 256), 0), iota((256, 256), 1)
    perm[...] = (c == ((r // 4) % 4) * 64 + (r // 16) * 4 + r % 4).astype(F32).astype(BF16)
    lane = iota((1, 128), 1)
    small[0].wait()
    for g in range(4):
        for t in range(8):
            a = pair_gate[(row // 4) * 4 + g, 4 * t + 2 * core].astype(F32)
            b = pair_gate[(row // 4) * 4 + g, 4 * t + 2 * core + 1].astype(F32)
            gate[g : g + 1, t * 128 : (t + 1) * 128] = jnp.where(lane < 64, a, b)

    def gated(ref, which):
        lane = iota((1, 256), 1)
        blocks = []
        for a in range(4):
            line = jnp.zeros((1, 256), F32)
            for b in range(4):
                line = jnp.where(lane // 64 == b, green_gate[which, a, b].astype(F32), line)
            blocks.append(ref[64 * a : 64 * a + 64, :].astype(F32) * line)
        return jnp.concatenate(blocks, axis=0)

    small[1].wait()
    small[2].wait()
    vt[...] = gated(virt, 1).T.astype(BF16)

    pl.semaphore_wait(barrier, 10)
    for there in lines:
        pl.semaphore_signal(ready.at[0], inc=1, device_id=there, device_id_type=MESH)
    for t in range(8):
        pltpu.make_async_remote_copy(
            src_ref=ints.at[:, :, tile(t, 1 - core)],
            dst_ref=mine.at[:, :, pl.ds(t * 128, 128)],
            send_sem=x_send,
            recv_sem=x_recv.at[t // 2],
            device_id=partner,
            device_id_type=MESH,
        ).start()

    def wait_for(ref, sem):
        pltpu.make_async_copy(ref, ref, sem).wait()

    def half(first, lanes):
        @pl.loop(0, 2)
        def _(n):
            k = first + n
            for g in range(4):
                rows = pl.ds(64 * g, 64)
                mx[k, rows, lanes] = (mx[k, rows, lanes].astype(F32) * gate[g : g + 1, lanes]).astype(BF16)
            hd[k, :, lanes] = jnp.dot(vt[...], mx[k, :, lanes], preferred_element_type=F32).astype(BF16)

    def pieces(start, width):
        return [(start + n, n) for n in range(0, width, QW)]

    def to_chips(src, dst, lanes, part):
        for g in range(4):
            got = jnp.dot(
                perm[...], src[:, pl.ds(64 * g, 64), lanes].reshape(256, QW), preferred_element_type=F32
            )
            dst[pl.ds(16 * g, 16), :, part] = got.astype(BF16).reshape(16, 16, QW)

    def send_all(src, dst, send_sem, recv_sem, only=None):
        @pl.loop(1, 64)
        def _(i):
            pos = other(i)

            def start():
                pltpu.make_async_remote_copy(
                    src_ref=src.at[chip_of(pos)],
                    dst_ref=dst.at[chip],
                    send_sem=send_sem,
                    recv_sem=recv_sem,
                    device_id=device(pos, core),
                    device_id_type=MESH,
                ).start()

            if only is None:
                start()
            else:
                apart = (i % 4) * ((i + i // 4) % 4) * ((i + i // 16) % 4)
                pl.when((apart == 0) if only == 0 else (apart != 0))(start)

    def send_h(n, only=None):
        send_all(hsend[n], hrecv[n], h_send.at[n], h_recv.at[n], only)
        if only != 1:
            hrecv[n][chip] = hsend[n][chip]

    def send_m(n):
        send_all(msend[n], mall[n].at[0], m_send.at[n], m_recv.at[n])
        mall[n][0, chip] = msend[n][chip]

    def wait_all(ref, sem):
        wait_for(ref.at[pl.ds(0, 63)], sem)

    wait_for(mine, x_own)
    for start, _ in pieces(0, 1024):
        half(2 * core, pl.ds(start, QW))

    def make_h(n):
        first, width = H_CHUNKS[n]
        for start, at in pieces(first, width):
            wait_for(mx.at[pl.ds(2 - 2 * core, 2), :, pl.ds(start, QW)], x_recv.at[start // QW])
            half(2 - 2 * core, pl.ds(start, QW))
            to_chips(hd, hsend[n], pl.ds(start, QW), pl.ds(at, QW))

    def make_m(n):
        first, width = M_CHUNKS[n]
        for start, at in pieces(first, width):
            to_chips(mx, msend[n], pl.ds(start, QW), pl.ds(at, QW))

    pl.semaphore_wait(ready.at[0], 9)
    for off in (1, 2, 3):
        there = device(along("z", off), core)
        pl.semaphore_signal(ready.at[1], inc=1, device_id=there, device_id_type=MESH)
    make_h(0)
    send_h(0, 0)
    make_h(1)
    pl.semaphore_wait(ready.at[1], 3)
    send_h(0, 1)
    send_h(1)
    for n in range(2, len(H_CHUNKS)):
        make_h(n)
        send_h(n)
    for n in range(len(M_CHUNKS)):
        make_m(n)
        if n < AHEAD:
            send_m(n)

    rr, cc = iota((1024, 256), 0), iota((1024, 256), 1)
    spread[...] = (
        cc == 32 * (rr // 128) + 16 * ((rr // 8) % 2) + 2 * ((rr // 16) % 8) + (rr // 4) % 2
    ).astype(F32).astype(BF16)
    small[3].wait()
    occ_t[...] = gated(occ, 0).astype(BF16)

    @pl.loop(0, 4)
    def _(k):
        rows = pl.ds(pl.multiple_of(k * 256, 256), 256)
        t1 = jnp.dot(spread[rows, :], occ_t[...], preferred_element_type=F32).astype(BF16)
        for n in range(4):
            got = lax.dot_general(
                t1, spread[n * 256 : (n + 1) * 256, :], (((1,), (1,)), ((), ())), preferred_element_type=F32
            )
            wide[rows, n * 256 : (n + 1) * 256] = jnp.where(r % 4 == c % 4, got, 0.0).astype(BF16)

    for n, (first, width) in enumerate(H_CHUNKS):
        wait_all(hrecv[n], h_recv.at[n])
        if n == len(H_CHUNKS) - 1 and AHEAD < len(M_CHUNKS):
            send_m(AHEAD)
        for start, at in pieces(first, width):
            t = start // 128
            for k in range(4):
                rows = pl.ds(k * 256, 256)
                got = jnp.dot(
                    wide[rows, :], hrecv[n][:, :, pl.ds(at, QW)].reshape(1024, QW), preferred_element_type=F32
                )
                both_t[t // 4, pl.ds(t % 4, 2), :, :, :, rows] = got.T.astype(BF16).reshape(2, 4, 2, 16, 256)

    def copies(t, phase):
        order = order_of(t)
        d1, d2 = dims_of(t)
        axis = order[phase]
        res = []
        for off in (2, 1, 3):
            k = (me[axis] + off) % 4
            if phase == 0:
                src = send_a.at[(t // 2,) + pick(DIMS, axis, k) + (slice(None), pl.ds((t % 2) * 128, 128))]
                dst = recv_a[t].at[off - 1]
            elif phase == 1:
                src, dst = send_b[t].at[pick(d1, axis, k)], recv_b[t].at[off - 1]
            else:
                src, dst = send_c[t].at[pick(d2, axis, k)], recv_c[t].at[off - 1]
            res.append(
                pltpu.make_async_remote_copy(
                    src_ref=src,
                    dst_ref=dst,
                    send_sem=r_send.at[min(phase, 1)],
                    recv_sem=r_recv.at[t, phase],
                    device_id=device(along(axis, off), core),
                    device_id_type=MESH,
                )
            )
        return res

    def launch(t, phase):
        for cp in copies(t, phase):
            cp.start()

    def launch_direct(t):
        _, one, two = order_of(t)
        d1, d2 = dims_of(t)
        for n in range(15, 0, -1):
            pos = along(one, n // 4)
            pos[two] = (me[two] + n % 4) % 4
            at = dict(zip(d1, pick(d1, one, pos[one])))
            at.update(zip(d2, pick(d2, two, pos[two])))
            pltpu.make_async_remote_copy(
                src_ref=send_b[t].at[tuple(at[d] for d in d1)],
                dst_ref=recv_d[t].at[n - 1],
                send_sem=r_send.at[1],
                recv_sem=r_recv.at[t, 1],
                device_id=device(pos, core),
                device_id_type=MESH,
            ).start()

    def phase_a(u):
        ch, whose, piece = UNITS[u]
        right = mall[ch][whose, :, :, pl.ds(piece * QW, QW)].reshape(1024, QW)
        for ylo in range(2):
            for x in (0, 2):
                left = both_t[ylo, x : x + 2].reshape(256, 1024)
                got = jnp.dot(left, right, preferred_element_type=F32).reshape(2, 4, 2, 16, QW)
                stage[ylo, x : x + 2] = got
                send_a[u, ylo, x : x + 2] = got.astype(BF16)
        for t in (2 * u, 2 * u + 1):
            launch(t, 0)
            axis = order_of(t)[0]
            acc_a[t][...] = stage[pick(DIMS, axis, me[axis]) + (slice(None), pl.ds((t % 2) * 128, 128))]

    def phase_b(t):
        wait_for(recv_a[t], r_recv.at[t, 0])
        total = acc_a[t][...]
        for off in (1, 2, 3):
            total += recv_a[t][off - 1].astype(F32)
        acc_a[t][...] = total
        send_b[t][...] = total.astype(send_b[t].dtype)
        if t in DIRECT_TILES:
            launch_direct(t)
        else:
            launch(t, 1)

    def phase_c(t):
        if t in DIRECT_TILES:
            return
        axis = order_of(t)[1]
        wait_for(recv_b[t], r_recv.at[t, 1])
        total = acc_a[t][pick(dims_of(t)[0], axis, me[axis])]
        for off in (1, 2, 3):
            total += recv_b[t][off - 1].astype(F32)
        acc_b[t][...] = total
        send_c[t][...] = total.astype(BF16)
        launch(t, 2)

    def finish(t):
        _, one, two = order_of(t)
        d1, d2 = dims_of(t)
        if t in DIRECT_TILES:
            wait_for(recv_d[t], r_recv.at[t, 1])
            at = dict(zip(d1, pick(d1, one, me[one])))
            at.update(zip(d2, pick(d2, two, me[two])))
            total = acc_a[t][tuple(at[d] for d in d1)]
            for n in range(15):
                total += recv_d[t][n].astype(F32)
        else:
            wait_for(recv_c[t], r_recv.at[t, 2])
            total = acc_b[t][pick(d2, two, me[two])]
            for off in (1, 2, 3):
                total += recv_c[t][off - 1].astype(F32)
        ch, whose, piece = UNITS[t // 2]
        at = (M_CHUNKS[ch][0] + piece * QW) // 128 + t % 2
        out[:, tile(at, core if whose == 0 else 1 - core)] = total * (1.0 / 256.0)

    def swap(ch):
        return pltpu.make_async_remote_copy(
            src_ref=mall[ch].at[0],
            dst_ref=mall[ch].at[1],
            send_sem=p_send.at[ch],
            recv_sem=p_recv.at[ch],
            device_id=partner,
            device_id_type=MESH,
        )

    for name, u in [(name, u) for name, first, last in PLAN for u in range(first, last)]:
        if name == "a":
            ch, whose, piece = UNITS[u]
            if piece == 0 and whose == 0:
                wait_all(mall[ch].at[0], m_recv.at[ch])
                if ch + AHEAD + 1 < len(M_CHUNKS):
                    send_m(ch + AHEAD + 1)
                swap(ch).start()
            if piece == 0 and whose == 1:
                swap(ch).wait_recv()
            phase_a(u)
        else:
            for t in (2 * u, 2 * u + 1):
                {"b": phase_b, "c": phase_c, "f": finish}[name](t)

    for n in range(len(H_CHUNKS)):
        wait_all(hsend[n], h_send.at[n])
    for n in range(len(M_CHUNKS)):
        wait_all(msend[n], m_send.at[n])
        swap(n).wait_send()
    wait_for(mine, x_send)
    wait_for(send_a.at[pl.ds(0, NT * 3 // 8)], r_send.at[0])
    wait_for(mx.at[pl.ds(0, 3), pl.ds(0, NT * 10)], r_send.at[1])


def local(integrals, occupied, virtual, pair_mask, green_mask):
    vmem = pltpu.VMEM
    dma = pltpu.SemaphoreType.DMA
    nh, nm = len(H_CHUNKS), len(M_CHUNKS)
    whole = shape_of(DIMS)
    d1 = [shape_of(dims_of(t)[0]) + (16, 128) for t in range(NT)]
    d2 = [shape_of(dims_of(t)[1]) + (16, 128) for t in range(NT)]
    scratch = [
        vmem((256, 256), BF16),
        vmem((256, 256), BF16),
        pltpu.SMEM((16, 32), jnp.int32),
        pltpu.SMEM((2, 4, 4), jnp.int32),
        vmem((4, 256, 1024), BF16),
        vmem((8, 1024), F32),
        vmem((256, 256), BF16),
        vmem((256, 256), BF16),
        vmem((4, 256, 1024), BF16),
        vmem((1024, 256), BF16),
        vmem((256, 256), BF16),
        vmem((1024, 1024), BF16),
        vmem(whole + (16, 1024), BF16),
        vmem(whole + (16, QW), F32),
        *[vmem((64, 16, w), BF16) for _, w in H_CHUNKS],
        *[vmem((64, 16, w), BF16) for _, w in H_CHUNKS],
        *[vmem((64, 16, w), BF16) for _, w in M_CHUNKS],
        *[vmem((2, 64, 16, w), BF16) for _, w in M_CHUNKS],
        vmem((len(UNITS),) + whole + (16, QW), BF16),
        *[vmem((3,) + s, BF16) for s in d1],
        *[vmem(s, F32) for s in d1],
        *[vmem(s, BF16) for s in d1],
        *[vmem((3,) + s, BF16) for s in d2],
        *[vmem(s, F32) for s in d2],
        *[vmem(s, BF16) for s in d2],
        *[vmem((3, 16, 128), BF16) for _ in d2],
        *[vmem((15, 16, 128), BF16) for _ in DIRECT_TILES],
        dma, dma, dma((4,)),
        dma((nh,)), dma((nh,)), dma((nm,)), dma((nm,)), dma((nm,)), dma((nm,)),
        dma((2,)), dma((NT, 3)), dma((4,)),
        pltpu.SemaphoreType.REGULAR((2,)),
    ]
    return pl.pallas_call(
        kernel,
        out_shape=jax.ShapeDtypeStruct((16, 2048), F32),
        in_specs=[pl.BlockSpec(memory_space=pltpu.HBM)] * 5,
        out_specs=pl.BlockSpec(memory_space=pltpu.VMEM),
        scratch_shapes=scratch,
        compiler_params=pltpu.CompilerParams(
            collective_id=0, has_side_effects=True, vmem_limit_bytes=61 * 2**20
        ),
        name="polarizability",
    )(integrals.reshape(2, 256, 2048), occupied, virtual, pair_mask, green_mask)


def solution(mesh):
    return jax.shard_map(
        local,
        mesh=mesh,
        in_specs=(P(("row", "col"), None), P(), P(), P(), P()),
        out_specs=P(("row", "col"), None),
        check_vma=False,
    )
```

```python
import functools

import jax
import jax.numpy as jnp
from jax import lax
from jax.experimental import pallas as pl
from jax.experimental.pallas import tpu as pltpu
from jax.sharding import PartitionSpec as P

F32 = jnp.float32
BF16 = jnp.bfloat16
MESH = pl.DeviceIdType.MESH
QW = 256
H_CHUNKS = ((0, 256), (256, 256), (512, 512))
M_CHUNKS = ((0, 256), (256, 256), (512, 512))
UNITS = tuple(
    (ch, whose, piece) for ch, (_, w) in enumerate(M_CHUNKS) for whose in range(2) for piece in range(w // QW)
)
NT = 2 * len(UNITS)
DIMS = ("ylo", "x", "z", "yhi")
SIZE = {"ylo": 2, "x": 4, "z": 4, "yhi": 2}
ORDERS = (("x", "y", "z"), ("y", "z", "x"), ("z", "x", "y"))


def parts_of(axis):
    return ("ylo", "yhi") if axis == "y" else (axis,)


def left_after(dims, axis):
    return tuple(d for d in dims if d not in parts_of(axis))


def pick(dims, axis, k):
    at = {"x": k, "z": k} if axis != "y" else {"ylo": k % 2, "yhi": k // 2}
    return tuple(at[d] if d in parts_of(axis) else slice(None) for d in dims)


def shape_of(dims):
    return tuple(SIZE[d] for d in dims)


def device(pos, core):
    return ((pos["y"] % 2) * 8 + pos["x"] * 2 + core, pos["z"] * 2 + pos["y"] // 2)


def iota(shape, axis):
    return lax.broadcasted_iota(jnp.int32, shape, axis)


def order_of(t):
    return ORDERS[t % 3]


def dims_of(t):
    d1 = left_after(DIMS, order_of(t)[0])
    return d1, left_after(d1, order_of(t)[1])


DIRECT = (6, 7)
AHEAD = len(M_CHUNKS)
PLAN = (("a", 0, 8), ("b", 0, 8), ("c", 0, 8), ("f", 0, 8))


DIRECT_TILES = tuple(2 * u + n for u in DIRECT for n in range(2))


def kernel(*refs):
    refs = list(refs)

    def take(n):
        got = refs[:n]
        del refs[:n]
        return got

    ints, occ_in, virt_in, pair_in, green_in, out = take(6)
    occ, virt, pair_gate, green_gate = take(4)
    mx, gate, vt, perm, hd, spread, occ_t, wide, both_t, stage = take(10)
    hsend, hrecv = take(len(H_CHUNKS)), take(len(H_CHUNKS))
    msend, mall = take(len(M_CHUNKS)), take(len(M_CHUNKS))
    (send_a,) = take(1)
    recv_a, acc_a, send_b, recv_b, acc_b, send_c, recv_c = (take(NT) for _ in range(7))
    recv_d = dict(zip(DIRECT_TILES, take(len(DIRECT_TILES))))
    x_own, x_send, x_recv, h_send, h_recv, m_send, m_recv, p_send, p_recv, r_send, r_recv, s_in, ready = refs
    row, col = lax.axis_index("row"), lax.axis_index("col")
    core = row % 2
    me = {"x": (row // 2) % 4, "y": (col % 2) * 2 + row // 8, "z": col // 2}
    chip = (row // 2) * 8 + col
    partner = (row - core + (1 - core), col)

    def along(axis, off):
        pos = dict(me)
        pos[axis] = (me[axis] + off) % 4
        return pos

    def other(i):
        return {
            "x": (me["x"] + i) % 4,
            "y": (me["y"] + i + i // 4) % 4,
            "z": (me["z"] + i + i // 16) % 4,
        }

    def chip_of(pos):
        return ((pos["y"] % 2) * 4 + pos["x"]) * 8 + pos["z"] * 2 + pos["y"] // 2

    barrier = pltpu.get_barrier_semaphore()
    pl.semaphore_signal(barrier, inc=1, device_id=partner, device_id_type=MESH)
    lines = [device(along(axis, off), core) for off in (2, 1, 3) for axis in ("x", "y", "z")]
    for there in lines:
        pl.semaphore_signal(barrier, inc=1, device_id=there, device_id_type=MESH)

    small = []
    for n, (src, dst) in enumerate(((pair_in, pair_gate), (green_in, green_gate), (virt_in, virt), (occ_in, occ))):
        cp = pltpu.make_async_copy(src, dst, s_in.at[n])
        cp.start()
        small.append(cp)

    def tile(t, c):
        return pl.ds(pl.multiple_of((2 * t + c) * 128, 128), 128)

    mine = mx.at[pl.ds(2 * core, 2)]
    for t in range(8):
        pltpu.make_async_copy(ints.at[:, :, tile(t, core)], mine.at[:, :, pl.ds(t * 128, 128)], x_own).start()

    r, c = iota((256, 256), 0), iota((256, 256), 1)
    perm[...] = (c == ((r // 4) % 4) * 64 + (r // 16) * 4 + r % 4).astype(F32).astype(BF16)
    lane = iota((1, 128), 1)
    small[0].wait()
    for g in range(4):
        for t in range(8):
            a = pair_gate[(row // 4) * 4 + g, 4 * t + 2 * core].astype(F32)
            b = pair_gate[(row // 4) * 4 + g, 4 * t + 2 * core + 1].astype(F32)
            gate[g : g + 1, t * 128 : (t + 1) * 128] = jnp.where(lane < 64, a, b)

    def gated(ref, which):
        lane = iota((1, 256), 1)
        blocks = []
        for a in range(4):
            line = jnp.zeros((1, 256), F32)
            for b in range(4):
                line = jnp.where(lane // 64 == b, green_gate[which, a, b].astype(F32), line)
            blocks.append(ref[64 * a : 64 * a + 64, :].astype(F32) * line)
        return jnp.concatenate(blocks, axis=0)

    small[1].wait()
    small[2].wait()
    vt[...] = gated(virt, 1).T.astype(BF16)

    pl.semaphore_wait(barrier, 10)
    for there in lines:
        pl.semaphore_signal(ready.at[0], inc=1, device_id=there, device_id_type=MESH)
    for t in range(8):
        pltpu.make_async_remote_copy(
            src_ref=ints.at[:, :, tile(t, 1 - core)],
            dst_ref=mine.at[:, :, pl.ds(t * 128, 128)],
            send_sem=x_send,
            recv_sem=x_recv.at[t // 2],
            device_id=partner,
            device_id_type=MESH,
        ).start()

    def wait_for(ref, sem):
        pltpu.make_async_copy(ref, ref, sem).wait()

    def half(first, lanes):
        @pl.loop(0, 2)
        def _(n):
            k = first + n
            for g in range(4):
                rows = pl.ds(64 * g, 64)
                mx[k, rows, lanes] = (mx[k, rows, lanes].astype(F32) * gate[g : g + 1, lanes]).astype(BF16)
            hd[k, :, lanes] = jnp.dot(vt[...], mx[k, :, lanes], preferred_element_type=F32).astype(BF16)

    def pieces(start, width):
        return [(start + n, n) for n in range(0, width, QW)]

    def to_chips(src, dst, lanes, part):
        for g in range(4):
            got = jnp.dot(
                perm[...], src[:, pl.ds(64 * g, 64), lanes].reshape(256, QW), preferred_element_type=F32
            )
            dst[pl.ds(16 * g, 16), :, part] = got.astype(BF16).reshape(16, 16, QW)

    def send_all(src, dst, send_sem, recv_sem, only=None):
        @pl.loop(1, 64)
        def _(i):
            pos = other(i)

            def start():
                pltpu.make_async_remote_copy(
                    src_ref=src.at[chip_of(pos)],
                    dst_ref=dst.at[chip],
                    send_sem=send_sem,
                    recv_sem=recv_sem,
                    device_id=device(pos, core),
                    device_id_type=MESH,
                ).start()

            if only is None:
                start()
            else:
                apart = (i % 4) * ((i + i // 4) % 4) * ((i + i // 16) % 4)
                pl.when((apart == 0) if only == 0 else (apart != 0))(start)

    def send_h(n, only=None):
        send_all(hsend[n], hrecv[n], h_send.at[n], h_recv.at[n], only)
        if only != 1:
            hrecv[n][chip] = hsend[n][chip]

    def send_m(n):
        send_all(msend[n], mall[n].at[0], m_send.at[n], m_recv.at[n])
        mall[n][0, chip] = msend[n][chip]

    def wait_all(ref, sem):
        wait_for(ref.at[pl.ds(0, 63)], sem)

    wait_for(mine, x_own)
    for start, _ in pieces(0, 1024):
        half(2 * core, pl.ds(start, QW))

    def make_h(n):
        first, width = H_CHUNKS[n]
        for start, at in pieces(first, width):
            wait_for(mx.at[pl.ds(2 - 2 * core, 2), :, pl.ds(start, QW)], x_recv.at[start // QW])
            half(2 - 2 * core, pl.ds(start, QW))
            to_chips(hd, hsend[n], pl.ds(start, QW), pl.ds(at, QW))

    def make_m(n):
        first, width = M_CHUNKS[n]
        for start, at in pieces(first, width):
            to_chips(mx, msend[n], pl.ds(start, QW), pl.ds(at, QW))

    make_h(0)
    pl.semaphore_wait(ready.at[0], 9)
    for off in (1, 2, 3):
        there = device(along("z", off), core)
        pl.semaphore_signal(ready.at[1], inc=1, device_id=there, device_id_type=MESH)
    send_h(0, 0)
    make_h(1)
    pl.semaphore_wait(ready.at[1], 3)
    send_h(0, 1)
    send_h(1)
    for n in range(2, len(H_CHUNKS)):
        make_h(n)
        send_h(n)
    for n in range(len(M_CHUNKS)):
        make_m(n)
        if n < AHEAD:
            send_m(n)

    rr, cc = iota((1024, 256), 0), iota((1024, 256), 1)
    spread[...] = (
        cc == 32 * (rr // 128) + 16 * ((rr // 8) % 2) + 2 * ((rr // 16) % 8) + (rr // 4) % 2
    ).astype(F32).astype(BF16)
    small[3].wait()
    occ_t[...] = gated(occ, 0).astype(BF16)

    @pl.loop(0, 4)
    def _(k):
        rows = pl.ds(pl.multiple_of(k * 256, 256), 256)
        t1 = jnp.dot(spread[rows, :], occ_t[...], preferred_element_type=F32).astype(BF16)
        for n in range(4):
            got = lax.dot_general(
                t1, spread[n * 256 : (n + 1) * 256, :], (((1,), (1,)), ((), ())), preferred_element_type=F32
            )
            wide[rows, n * 256 : (n + 1) * 256] = jnp.where(r % 4 == c % 4, got, 0.0).astype(BF16)

    for n, (first, width) in enumerate(H_CHUNKS):
        wait_all(hrecv[n], h_recv.at[n])
        if n == len(H_CHUNKS) - 1 and AHEAD < len(M_CHUNKS):
            send_m(AHEAD)
        for start, at in pieces(first, width):
            t = start // 128
            for k in range(4):
                rows = pl.ds(k * 256, 256)
                got = jnp.dot(
                    wide[rows, :], hrecv[n][:, :, pl.ds(at, QW)].reshape(1024, QW), preferred_element_type=F32
                )
                both_t[t // 4, pl.ds(t % 4, 2), :, :, :, rows] = got.T.astype(BF16).reshape(2, 4, 2, 16, 256)

    def copies(t, phase):
        order = order_of(t)
        d1, d2 = dims_of(t)
        axis = order[phase]
        res = []
        for off in (2, 1, 3):
            k = (me[axis] + off) % 4
            if phase == 0:
                src = send_a.at[(t // 2,) + pick(DIMS, axis, k) + (slice(None), pl.ds((t % 2) * 128, 128))]
                dst = recv_a[t].at[off - 1]
            elif phase == 1:
                src, dst = send_b[t].at[pick(d1, axis, k)], recv_b[t].at[off - 1]
            else:
                src, dst = send_c[t].at[pick(d2, axis, k)], recv_c[t].at[off - 1]
            res.append(
                pltpu.make_async_remote_copy(
                    src_ref=src,
                    dst_ref=dst,
                    send_sem=r_send.at[min(phase, 1)],
                    recv_sem=r_recv.at[t, phase],
                    device_id=device(along(axis, off), core),
                    device_id_type=MESH,
                )
            )
        return res

    def launch(t, phase):
        for cp in copies(t, phase):
            cp.start()

    def launch_direct(t):
        _, one, two = order_of(t)
        d1, d2 = dims_of(t)
        for n in range(15, 0, -1):
            pos = along(one, n // 4)
            pos[two] = (me[two] + n % 4) % 4
            at = dict(zip(d1, pick(d1, one, pos[one])))
            at.update(zip(d2, pick(d2, two, pos[two])))
            pltpu.make_async_remote_copy(
                src_ref=send_b[t].at[tuple(at[d] for d in d1)],
                dst_ref=recv_d[t].at[n - 1],
                send_sem=r_send.at[1],
                recv_sem=r_recv.at[t, 1],
                device_id=device(pos, core),
                device_id_type=MESH,
            ).start()

    def phase_a(u):
        ch, whose, piece = UNITS[u]
        right = mall[ch][whose, :, :, pl.ds(piece * QW, QW)].reshape(1024, QW)
        for ylo in range(2):
            for x in (0, 2):
                left = both_t[ylo, x : x + 2].reshape(256, 1024)
                got = jnp.dot(left, right, preferred_element_type=F32).reshape(2, 4, 2, 16, QW)
                stage[ylo, x : x + 2] = got
                send_a[u, ylo, x : x + 2] = got.astype(BF16)
        for t in (2 * u, 2 * u + 1):
            launch(t, 0)
            axis = order_of(t)[0]
            acc_a[t][...] = stage[pick(DIMS, axis, me[axis]) + (slice(None), pl.ds((t % 2) * 128, 128))]

    def phase_b(t):
        wait_for(recv_a[t], r_recv.at[t, 0])
        total = acc_a[t][...]
        for off in (1, 2, 3):
            total += recv_a[t][off - 1].astype(F32)
        acc_a[t][...] = total
        send_b[t][...] = total.astype(send_b[t].dtype)
        if t in DIRECT_TILES:
            launch_direct(t)
        else:
            launch(t, 1)

    def phase_c(t):
        if t in DIRECT_TILES:
            return
        axis = order_of(t)[1]
        wait_for(recv_b[t], r_recv.at[t, 1])
        total = acc_a[t][pick(dims_of(t)[0], axis, me[axis])]
        for off in (1, 2, 3):
            total += recv_b[t][off - 1].astype(F32)
        acc_b[t][...] = total
        send_c[t][...] = total.astype(BF16)
        launch(t, 2)

    def finish(t):
        _, one, two = order_of(t)
        d1, d2 = dims_of(t)
        if t in DIRECT_TILES:
            wait_for(recv_d[t], r_recv.at[t, 1])
            at = dict(zip(d1, pick(d1, one, me[one])))
            at.update(zip(d2, pick(d2, two, me[two])))
            total = acc_a[t][tuple(at[d] for d in d1)]
            for n in range(15):
                total += recv_d[t][n].astype(F32)
        else:
            wait_for(recv_c[t], r_recv.at[t, 2])
            total = acc_b[t][pick(d2, two, me[two])]
            for off in (1, 2, 3):
                total += recv_c[t][off - 1].astype(F32)
        ch, whose, piece = UNITS[t // 2]
        at = (M_CHUNKS[ch][0] + piece * QW) // 128 + t % 2
        out[:, tile(at, core if whose == 0 else 1 - core)] = total * (1.0 / 256.0)

    def swap(ch):
        return pltpu.make_async_remote_copy(
            src_ref=mall[ch].at[0],
            dst_ref=mall[ch].at[1],
            send_sem=p_send.at[ch],
            recv_sem=p_recv.at[ch],
            device_id=partner,
            device_id_type=MESH,
        )

    for name, u in [(name, u) for name, first, last in PLAN for u in range(first, last)]:
        if name == "a":
            ch, whose, piece = UNITS[u]
            if piece == 0 and whose == 0:
                wait_all(mall[ch].at[0], m_recv.at[ch])
                if ch + AHEAD + 1 < len(M_CHUNKS):
                    send_m(ch + AHEAD + 1)
                swap(ch).start()
            if piece == 0 and whose == 1:
                swap(ch).wait_recv()
            phase_a(u)
        else:
            for t in (2 * u, 2 * u + 1):
                {"b": phase_b, "c": phase_c, "f": finish}[name](t)

    for n in range(len(H_CHUNKS)):
        wait_all(hsend[n], h_send.at[n])
    for n in range(len(M_CHUNKS)):
        wait_all(msend[n], m_send.at[n])
        swap(n).wait_send()
    wait_for(mine, x_send)
    wait_for(send_a.at[pl.ds(0, NT * 3 // 8)], r_send.at[0])
    wait_for(mx.at[pl.ds(0, 3), pl.ds(0, NT * 10)], r_send.at[1])


def local(integrals, occupied, virtual, pair_mask, green_mask):
    vmem = pltpu.VMEM
    dma = pltpu.SemaphoreType.DMA
    nh, nm = len(H_CHUNKS), len(M_CHUNKS)
    whole = shape_of(DIMS)
    d1 = [shape_of(dims_of(t)[0]) + (16, 128) for t in range(NT)]
    d2 = [shape_of(dims_of(t)[1]) + (16, 128) for t in range(NT)]
    scratch = [
        vmem((256, 256), BF16),
        vmem((256, 256), BF16),
        pltpu.SMEM((16, 32), jnp.int32),
        pltpu.SMEM((2, 4, 4), jnp.int32),
        vmem((4, 256, 1024), BF16),
        vmem((8, 1024), F32),
        vmem((256, 256), BF16),
        vmem((256, 256), BF16),
        vmem((4, 256, 1024), BF16),
        vmem((1024, 256), BF16),
        vmem((256, 256), BF16),
        vmem((1024, 1024), BF16),
        vmem(whole + (16, 1024), BF16),
        vmem(whole + (16, QW), F32),
        *[vmem((64, 16, w), BF16) for _, w in H_CHUNKS],
        *[vmem((64, 16, w), BF16) for _, w in H_CHUNKS],
        *[vmem((64, 16, w), BF16) for _, w in M_CHUNKS],
        *[vmem((2, 64, 16, w), BF16) for _, w in M_CHUNKS],
        vmem((len(UNITS),) + whole + (16, QW), BF16),
        *[vmem((3,) + s, BF16) for s in d1],
        *[vmem(s, F32) for s in d1],
        *[vmem(s, BF16) for s in d1],
        *[vmem((3,) + s, BF16) for s in d2],
        *[vmem(s, F32) for s in d2],
        *[vmem(s, BF16) for s in d2],
        *[vmem((3, 16, 128), BF16) for _ in d2],
        *[vmem((15, 16, 128), BF16) for _ in DIRECT_TILES],
        dma, dma, dma((4,)),
        dma((nh,)), dma((nh,)), dma((nm,)), dma((nm,)), dma((nm,)), dma((nm,)),
        dma((2,)), dma((NT, 3)), dma((4,)),
        pltpu.SemaphoreType.REGULAR((2,)),
    ]
    return pl.pallas_call(
        kernel,
        out_shape=jax.ShapeDtypeStruct((16, 2048), F32),
        in_specs=[pl.BlockSpec(memory_space=pltpu.HBM)] * 5,
        out_specs=pl.BlockSpec(memory_space=pltpu.VMEM),
        scratch_shapes=scratch,
        compiler_params=pltpu.CompilerParams(
            collective_id=0, has_side_effects=True, vmem_limit_bytes=61 * 2**20
        ),
        name="polarizability",
    )(integrals.reshape(2, 256, 2048), occupied, virtual, pair_mask, green_mask)


def solution(mesh):
    return jax.shard_map(
        local,
        mesh=mesh,
        in_specs=(P(("row", "col"), None), P(), P(), P(), P()),
        out_specs=P(("row", "col"), None),
        check_vma=False,
    )
```

```python
import functools

import jax
import jax.numpy as jnp
from jax import lax
from jax.experimental import pallas as pl
from jax.experimental.pallas import tpu as pltpu
from jax.sharding import PartitionSpec as P

F32 = jnp.float32
BF16 = jnp.bfloat16
MESH = pl.DeviceIdType.MESH
QW = 256
H_CHUNKS = ((0, 256), (256, 256), (512, 512))
M_CHUNKS = ((0, 512), (512, 512))
UNITS = tuple(
    (ch, whose, piece) for ch, (_, w) in enumerate(M_CHUNKS) for whose in range(2) for piece in range(w // QW)
)
NT = 2 * len(UNITS)
DIMS = ("ylo", "x", "z", "yhi")
SIZE = {"ylo": 2, "x": 4, "z": 4, "yhi": 2}
ORDERS = (("x", "y", "z"), ("y", "z", "x"), ("z", "x", "y"))


def parts_of(axis):
    return ("ylo", "yhi") if axis == "y" else (axis,)


def left_after(dims, axis):
    return tuple(d for d in dims if d not in parts_of(axis))


def pick(dims, axis, k):
    at = {"x": k, "z": k} if axis != "y" else {"ylo": k % 2, "yhi": k // 2}
    return tuple(at[d] if d in parts_of(axis) else slice(None) for d in dims)


def shape_of(dims):
    return tuple(SIZE[d] for d in dims)


def device(pos, core):
    return ((pos["y"] % 2) * 8 + pos["x"] * 2 + core, pos["z"] * 2 + pos["y"] // 2)


def iota(shape, axis):
    return lax.broadcasted_iota(jnp.int32, shape, axis)


def order_of(t):
    return ORDERS[t % 3]


def dims_of(t):
    d1 = left_after(DIMS, order_of(t)[0])
    return d1, left_after(d1, order_of(t)[1])


DIRECT = (4, 5, 6, 7)
AHEAD = len(M_CHUNKS)
PLAN = (("a", 0, 8), ("b", 0, 8), ("c", 0, 8), ("f", 0, 8))


DIRECT_TILES = tuple(2 * u + n for u in DIRECT for n in range(2))


def kernel(*refs):
    refs = list(refs)

    def take(n):
        got = refs[:n]
        del refs[:n]
        return got

    ints, occ_in, virt_in, pair_in, green_in, out = take(6)
    occ, virt, pair_gate, green_gate = take(4)
    mx, gate, vt, perm, hd, spread, occ_t, wide, both_t, stage = take(10)
    hsend, hrecv = take(len(H_CHUNKS)), take(len(H_CHUNKS))
    msend, mall = take(len(M_CHUNKS)), take(len(M_CHUNKS))
    (send_a,) = take(1)
    recv_a, acc_a, send_b, recv_b, acc_b, send_c, recv_c = (take(NT) for _ in range(7))
    recv_d = dict(zip(DIRECT_TILES, take(len(DIRECT_TILES))))
    x_own, x_send, x_recv, h_send, h_recv, m_send, m_recv, p_send, p_recv, r_send, r_recv, s_in, ready = refs
    row, col = lax.axis_index("row"), lax.axis_index("col")
    core = row % 2
    me = {"x": (row // 2) % 4, "y": (col % 2) * 2 + row // 8, "z": col // 2}
    chip = (row // 2) * 8 + col
    partner = (row - core + (1 - core), col)

    def along(axis, off):
        pos = dict(me)
        pos[axis] = (me[axis] + off) % 4
        return pos

    def other(i):
        return {
            "x": (me["x"] + i) % 4,
            "y": (me["y"] + i + i // 4) % 4,
            "z": (me["z"] + i + i // 16) % 4,
        }

    def chip_of(pos):
        return ((pos["y"] % 2) * 4 + pos["x"]) * 8 + pos["z"] * 2 + pos["y"] // 2

    barrier = pltpu.get_barrier_semaphore()
    pl.semaphore_signal(barrier, inc=1, device_id=partner, device_id_type=MESH)
    lines = [device(along(axis, off), core) for off in (2, 1, 3) for axis in ("x", "y", "z")]
    for there in lines:
        pl.semaphore_signal(barrier, inc=1, device_id=there, device_id_type=MESH)

    small = []
    for n, (src, dst) in enumerate(((pair_in, pair_gate), (green_in, green_gate), (virt_in, virt), (occ_in, occ))):
        cp = pltpu.make_async_copy(src, dst, s_in.at[n])
        cp.start()
        small.append(cp)

    def tile(t, c):
        return pl.ds(pl.multiple_of((2 * t + c) * 128, 128), 128)

    mine = mx.at[pl.ds(2 * core, 2)]
    for t in range(8):
        pltpu.make_async_copy(ints.at[:, :, tile(t, core)], mine.at[:, :, pl.ds(t * 128, 128)], x_own).start()

    r, c = iota((256, 256), 0), iota((256, 256), 1)
    perm[...] = (c == ((r // 4) % 4) * 64 + (r // 16) * 4 + r % 4).astype(F32).astype(BF16)
    lane = iota((1, 128), 1)
    small[0].wait()
    for g in range(4):
        for t in range(8):
            a = pair_gate[(row // 4) * 4 + g, 4 * t + 2 * core].astype(F32)
            b = pair_gate[(row // 4) * 4 + g, 4 * t + 2 * core + 1].astype(F32)
            gate[g : g + 1, t * 128 : (t + 1) * 128] = jnp.where(lane < 64, a, b)

    def gated(ref, which):
        lane = iota((1, 256), 1)
        blocks = []
        for a in range(4):
            line = jnp.zeros((1, 256), F32)
            for b in range(4):
                line = jnp.where(lane // 64 == b, green_gate[which, a, b].astype(F32), line)
            blocks.append(ref[64 * a : 64 * a + 64, :].astype(F32) * line)
        return jnp.concatenate(blocks, axis=0)

    small[1].wait()
    small[2].wait()
    vt[...] = gated(virt, 1).T.astype(BF16)

    pl.semaphore_wait(barrier, 10)
    for there in lines:
        pl.semaphore_signal(ready.at[0], inc=1, device_id=there, device_id_type=MESH)
    for t in range(8):
        pltpu.make_async_remote_copy(
            src_ref=ints.at[:, :, tile(t, 1 - core)],
            dst_ref=mine.at[:, :, pl.ds(t * 128, 128)],
            send_sem=x_send,
            recv_sem=x_recv.at[t // 2],
            device_id=partner,
            device_id_type=MESH,
        ).start()

    def wait_for(ref, sem):
        pltpu.make_async_copy(ref, ref, sem).wait()

    def half(first, lanes):
        @pl.loop(0, 2)
        def _(n):
            k = first + n
            for g in range(4):
                rows = pl.ds(64 * g, 64)
                mx[k, rows, lanes] = (mx[k, rows, lanes].astype(F32) * gate[g : g + 1, lanes]).astype(BF16)
            hd[k, :, lanes] = jnp.dot(vt[...], mx[k, :, lanes], preferred_element_type=F32).astype(BF16)

    def pieces(start, width):
        return [(start + n, n) for n in range(0, width, QW)]

    def to_chips(src, dst, lanes, part):
        for g in range(4):
            got = jnp.dot(
                perm[...], src[:, pl.ds(64 * g, 64), lanes].reshape(256, QW), preferred_element_type=F32
            )
            dst[pl.ds(16 * g, 16), :, part] = got.astype(BF16).reshape(16, 16, QW)

    def send_all(src, dst, send_sem, recv_sem, only=None):
        @pl.loop(1, 64)
        def _(i):
            pos = other(i)

            def start():
                pltpu.make_async_remote_copy(
                    src_ref=src.at[chip_of(pos)],
                    dst_ref=dst.at[chip],
                    send_sem=send_sem,
                    recv_sem=recv_sem,
                    device_id=device(pos, core),
                    device_id_type=MESH,
                ).start()

            if only is None:
                start()
            else:
                apart = (i % 4) * ((i + i // 4) % 4) * ((i + i // 16) % 4)
                pl.when((apart == 0) if only == 0 else (apart != 0))(start)

    def send_h(n, only=None):
        send_all(hsend[n], hrecv[n], h_send.at[n], h_recv.at[n], only)
        if only != 1:
            hrecv[n][chip] = hsend[n][chip]

    def send_m(n):
        send_all(msend[n], mall[n].at[0], m_send.at[n], m_recv.at[n])
        mall[n][0, chip] = msend[n][chip]

    def wait_all(ref, sem):
        wait_for(ref.at[pl.ds(0, 63)], sem)

    wait_for(mine, x_own)
    for start, _ in pieces(0, 1024):
        half(2 * core, pl.ds(start, QW))

    def make_h(n):
        first, width = H_CHUNKS[n]
        for start, at in pieces(first, width):
            wait_for(mx.at[pl.ds(2 - 2 * core, 2), :, pl.ds(start, QW)], x_recv.at[start // QW])
            half(2 - 2 * core, pl.ds(start, QW))
            to_chips(hd, hsend[n], pl.ds(start, QW), pl.ds(at, QW))

    def make_m(n):
        first, width = M_CHUNKS[n]
        for start, at in pieces(first, width):
            to_chips(mx, msend[n], pl.ds(start, QW), pl.ds(at, QW))

    pl.semaphore_wait(ready.at[0], 9)
    for off in (1, 2, 3):
        there = device(along("z", off), core)
        pl.semaphore_signal(ready.at[1], inc=1, device_id=there, device_id_type=MESH)
    make_h(0)
    send_h(0, 0)
    make_h(1)
    pl.semaphore_wait(ready.at[1], 3)
    send_h(0, 1)
    send_h(1)
    for n in range(2, len(H_CHUNKS)):
        make_h(n)
        send_h(n)
    for n in range(len(M_CHUNKS)):
        make_m(n)
        if n < AHEAD:
            send_m(n)

    rr, cc = iota((1024, 256), 0), iota((1024, 256), 1)
    spread[...] = (
        cc == 32 * (rr // 128) + 16 * ((rr // 8) % 2) + 2 * ((rr // 16) % 8) + (rr // 4) % 2
    ).astype(F32).astype(BF16)
    small[3].wait()
    occ_t[...] = gated(occ, 0).astype(BF16)

    @pl.loop(0, 4)
    def _(k):
        rows = pl.ds(pl.multiple_of(k * 256, 256), 256)
        t1 = jnp.dot(spread[rows, :], occ_t[...], preferred_element_type=F32).astype(BF16)
        for n in range(4):
            got = lax.dot_general(
                t1, spread[n * 256 : (n + 1) * 256, :], (((1,), (1,)), ((), ())), preferred_element_type=F32
            )
            wide[rows, n * 256 : (n + 1) * 256] = jnp.where(r % 4 == c % 4, got, 0.0).astype(BF16)

    for n, (first, width) in enumerate(H_CHUNKS):
        wait_all(hrecv[n], h_recv.at[n])
        if n == len(H_CHUNKS) - 1 and AHEAD < len(M_CHUNKS):
            send_m(AHEAD)
        for start, at in pieces(first, width):
            t = start // 128
            for k in range(4):
                rows = pl.ds(k * 256, 256)
                got = jnp.dot(
                    wide[rows, :], hrecv[n][:, :, pl.ds(at, QW)].reshape(1024, QW), preferred_element_type=F32
                )
                both_t[t // 4, pl.ds(t % 4, 2), :, :, :, rows] = got.T.astype(BF16).reshape(2, 4, 2, 16, 256)

    def copies(t, phase):
        order = order_of(t)
        d1, d2 = dims_of(t)
        axis = order[phase]
        res = []
        for off in (2, 1, 3):
            k = (me[axis] + off) % 4
            if phase == 0:
                src = send_a.at[(t // 2,) + pick(DIMS, axis, k) + (slice(None), pl.ds((t % 2) * 128, 128))]
                dst = recv_a[t].at[off - 1]
            elif phase == 1:
                src, dst = send_b[t].at[pick(d1, axis, k)], recv_b[t].at[off - 1]
            else:
                src, dst = send_c[t].at[pick(d2, axis, k)], recv_c[t].at[off - 1]
            res.append(
                pltpu.make_async_remote_copy(
                    src_ref=src,
                    dst_ref=dst,
                    send_sem=r_send.at[min(phase, 1)],
                    recv_sem=r_recv.at[t, phase],
                    device_id=device(along(axis, off), core),
                    device_id_type=MESH,
                )
            )
        return res

    def launch(t, phase):
        for cp in copies(t, phase):
            cp.start()

    def launch_direct(t):
        _, one, two = order_of(t)
        d1, d2 = dims_of(t)
        for n in range(15, 0, -1):
            pos = along(one, n // 4)
            pos[two] = (me[two] + n % 4) % 4
            at = dict(zip(d1, pick(d1, one, pos[one])))
            at.update(zip(d2, pick(d2, two, pos[two])))
            pltpu.make_async_remote_copy(
                src_ref=send_b[t].at[tuple(at[d] for d in d1)],
                dst_ref=recv_d[t].at[n - 1],
                send_sem=r_send.at[1],
                recv_sem=r_recv.at[t, 1],
                device_id=device(pos, core),
                device_id_type=MESH,
            ).start()

    def phase_a(u):
        ch, whose, piece = UNITS[u]
        right = mall[ch][whose, :, :, pl.ds(piece * QW, QW)].reshape(1024, QW)
        for ylo in range(2):
            for x in (0, 2):
                left = both_t[ylo, x : x + 2].reshape(256, 1024)
                got = jnp.dot(left, right, preferred_element_type=F32).reshape(2, 4, 2, 16, QW)
                stage[ylo, x : x + 2] = got
                send_a[u, ylo, x : x + 2] = got.astype(BF16)
        for t in (2 * u, 2 * u + 1):
            launch(t, 0)
            axis = order_of(t)[0]
            acc_a[t][...] = stage[pick(DIMS, axis, me[axis]) + (slice(None), pl.ds((t % 2) * 128, 128))]

    def phase_b(t):
        wait_for(recv_a[t], r_recv.at[t, 0])
        total = acc_a[t][...]
        for off in (1, 2, 3):
            total += recv_a[t][off - 1].astype(F32)
        acc_a[t][...] = total
        send_b[t][...] = total.astype(send_b[t].dtype)
        if t in DIRECT_TILES:
            launch_direct(t)
        else:
            launch(t, 1)

    def phase_c(t):
        if t in DIRECT_TILES:
            return
        axis = order_of(t)[1]
        wait_for(recv_b[t], r_recv.at[t, 1])
        total = acc_a[t][pick(dims_of(t)[0], axis, me[axis])]
        for off in (1, 2, 3):
            total += recv_b[t][off - 1].astype(F32)
        acc_b[t][...] = total
        send_c[t][...] = total.astype(BF16)
        launch(t, 2)

    def finish(t):
        _, one, two = order_of(t)
        d1, d2 = dims_of(t)
        if t in DIRECT_TILES:
            wait_for(recv_d[t], r_recv.at[t, 1])
            at = dict(zip(d1, pick(d1, one, me[one])))
            at.update(zip(d2, pick(d2, two, me[two])))
            total = acc_a[t][tuple(at[d] for d in d1)]
            for n in range(15):
                total += recv_d[t][n].astype(F32)
        else:
            wait_for(recv_c[t], r_recv.at[t, 2])
            total = acc_b[t][pick(d2, two, me[two])]
            for off in (1, 2, 3):
                total += recv_c[t][off - 1].astype(F32)
        ch, whose, piece = UNITS[t // 2]
        at = (M_CHUNKS[ch][0] + piece * QW) // 128 + t % 2
        out[:, tile(at, core if whose == 0 else 1 - core)] = total * (1.0 / 256.0)

    def swap(ch):
        return pltpu.make_async_remote_copy(
            src_ref=mall[ch].at[0],
            dst_ref=mall[ch].at[1],
            send_sem=p_send.at[ch],
            recv_sem=p_recv.at[ch],
            device_id=partner,
            device_id_type=MESH,
        )

    for name, u in [(name, u) for name, first, last in PLAN for u in range(first, last)]:
        if name == "a":
            ch, whose, piece = UNITS[u]
            if piece == 0 and whose == 0:
                wait_all(mall[ch].at[0], m_recv.at[ch])
                if ch + AHEAD + 1 < len(M_CHUNKS):
                    send_m(ch + AHEAD + 1)
                swap(ch).start()
            if piece == 0 and whose == 1:
                swap(ch).wait_recv()
            phase_a(u)
        else:
            for t in (2 * u, 2 * u + 1):
                {"b": phase_b, "c": phase_c, "f": finish}[name](t)

    for n in range(len(H_CHUNKS)):
        wait_all(hsend[n], h_send.at[n])
    for n in range(len(M_CHUNKS)):
        wait_all(msend[n], m_send.at[n])
        swap(n).wait_send()
    wait_for(mine, x_send)
    wait_for(send_a.at[pl.ds(0, NT * 3 // 8)], r_send.at[0])
    wait_for(mx.at[pl.ds(0, 3), pl.ds(0, NT * 10)], r_send.at[1])


def local(integrals, occupied, virtual, pair_mask, green_mask):
    vmem = pltpu.VMEM
    dma = pltpu.SemaphoreType.DMA
    nh, nm = len(H_CHUNKS), len(M_CHUNKS)
    whole = shape_of(DIMS)
    d1 = [shape_of(dims_of(t)[0]) + (16, 128) for t in range(NT)]
    d2 = [shape_of(dims_of(t)[1]) + (16, 128) for t in range(NT)]
    scratch = [
        vmem((256, 256), BF16),
        vmem((256, 256), BF16),
        pltpu.SMEM((16, 32), jnp.int32),
        pltpu.SMEM((2, 4, 4), jnp.int32),
        vmem((4, 256, 1024), BF16),
        vmem((8, 1024), F32),
        vmem((256, 256), BF16),
        vmem((256, 256), BF16),
        vmem((4, 256, 1024), BF16),
        vmem((1024, 256), BF16),
        vmem((256, 256), BF16),
        vmem((1024, 1024), BF16),
        vmem(whole + (16, 1024), BF16),
        vmem(whole + (16, QW), F32),
        *[vmem((64, 16, w), BF16) for _, w in H_CHUNKS],
        *[vmem((64, 16, w), BF16) for _, w in H_CHUNKS],
        *[vmem((64, 16, w), BF16) for _, w in M_CHUNKS],
        *[vmem((2, 64, 16, w), BF16) for _, w in M_CHUNKS],
        vmem((len(UNITS),) + whole + (16, QW), BF16),
        *[vmem((3,) + s, BF16) for s in d1],
        *[vmem(s, F32) for s in d1],
        *[vmem(s, BF16) for s in d1],
        *[vmem((3,) + s, BF16) for s in d2],
        *[vmem(s, F32) for s in d2],
        *[vmem(s, BF16) for s in d2],
        *[vmem((3, 16, 128), BF16) for _ in d2],
        *[vmem((15, 16, 128), BF16) for _ in DIRECT_TILES],
        dma, dma, dma((4,)),
        dma((nh,)), dma((nh,)), dma((nm,)), dma((nm,)), dma((nm,)), dma((nm,)),
        dma((2,)), dma((NT, 3)), dma((4,)),
        pltpu.SemaphoreType.REGULAR((2,)),
    ]
    return pl.pallas_call(
        kernel,
        out_shape=jax.ShapeDtypeStruct((16, 2048), F32),
        in_specs=[pl.BlockSpec(memory_space=pltpu.HBM)] * 5,
        out_specs=pl.BlockSpec(memory_space=pltpu.VMEM),
        scratch_shapes=scratch,
        compiler_params=pltpu.CompilerParams(
            collective_id=0, has_side_effects=True, vmem_limit_bytes=61 * 2**20
        ),
        name="polarizability",
    )(integrals.reshape(2, 256, 2048), occupied, virtual, pair_mask, green_mask)


def solution(mesh):
    return jax.shard_map(
        local,
        mesh=mesh,
        in_specs=(P(("row", "col"), None), P(), P(), P(), P()),
        out_specs=P(("row", "col"), None),
        check_vma=False,
    )
```
